128 devices in a mesh: scen: 16 (over y_hi, z, core), dec: 8 (over y_lo, x).
Axes of the slice: x: 4, y: 4 (y_hi: 2, y_lo: 2; y = y_hi * 2 + y_lo), z: 4, core: 2. Of those that a mesh axis runs over, the one named last changes fastest.
Arguments:
- order_qty: bfloat16 [8192, 8192], P('dec', 'scen'), may hold values from 0 to 2
- multiplier: float32 [8192, 8192], P('dec', 'scen'), may hold values from -6 to 6
- unit_cost: bfloat16 [8192, 8192], P('dec', 'scen'), may hold values from -6 to 6
- demand: bfloat16 [2048, 8192], P('dec', 'scen'), may hold values from -6 to 6
- technology: bfloat16 [8192, 2048], P('dec'), may hold values from -0.0625 to 0.0625
- kkt_inverse: bfloat16 [2048, 2048], P('dec'), may hold values from -1 to 3
- probability: float32 [8192], P('scen'), may hold values from 0.1 to 1
- scenario_node: int32 [8192, 1], P('scen'), may hold values from 0 to 511
Outputs:
- planned: bfloat16 [8192, 8192], P('dec', 'scen')
- recourse: bfloat16 [2048, 8192], P('dec', 'scen')
- consensus: float32 [8192, 512], P('dec')
- multiplier_next: float32 [8192, 8192], P('dec', 'scen')
The draws below stay inside these ranges and needn't reach their ends.
Inputs may be any that keep to these rules, and one draw needn't show every extreme that they name: `scenario_node`: every one of the 512 nodes is the node of some scenario.
All inputs are finite; a program needn't handle non-finite values.
Results may differ from the reference program's by a relative error of at most 0.023.
Values may be sent and summed in bfloat16 or wider, within the bound.
A program may use at most 64 MiB of HBM per device.

```python
import math
import jax
import jax.numpy as jnp
from jax import lax

NX = 8192
M = 2048
G = 512
SCEN = 8192


def draw_kkt_inverse(key, part):
    first, second = jax.random.split(key)
    base = jnp.clip(jax.random.normal(first, (M, M), jnp.float32), -4.0, 4.0)
    offdiag = (base + base.T) * (0.5 / jnp.sqrt(jnp.float32(M)))
    diagonal = jax.random.uniform(second, (M,), jnp.float32, 1.0, 2.0)
    return (offdiag + jnp.diag(diagonal)).astype(jnp.bfloat16)


def steps_of(rng, dims, pieces, low, top_value):
    loudness = 1.0
    for axis_at, blocks in pieces:
        heights = jax.random.uniform(jax.random.fold_in(jax.random.fold_in(rng, 6), axis_at), (blocks,), jnp.float32, low / len(pieces), top_value / len(pieces))
        loudness = loudness * jnp.repeat(jnp.exp(heights), dims[axis_at] // blocks).reshape((-1,) + (1,) * (len(dims) - 1 - axis_at))
    return loudness


def different_ones(rng, rows, count, top, lift):
    order = jax.random.permutation(jax.random.fold_in(rng, 1), count)
    favour = order
    for power in range(3):
        favour = favour * favour // count
    favour = favour * lift // count
    chance = jax.random.randint(jax.random.fold_in(rng, 2), (rows, count), 0, 4096) + favour
    sure = jax.random.permutation(jax.random.fold_in(rng, 3), rows)[jnp.arange(count) % rows]
    chance = jnp.where(jnp.arange(rows)[:, None] == sure[None, :], 1 << 14, chance)
    merit = chance * count + jnp.arange(count)
    return lax.top_k(merit.astype(jnp.int32), top)[1].astype(jnp.int32)


def scatter_about(stream_key, extent, spread, most, shards=(), kind=jnp.bfloat16):
    array = spread * jax.random.normal(stream_key, extent, jnp.float32)
    if shards:
        array = array * steps_of(stream_key, extent, shards, -0.22, 0.18)
    return jnp.clip(array, -most, most).astype(kind)


def setup_inputs(seed: int = 0) -> dict:
    arg_keys = jax.random.split(jax.random.key(seed), 9)
    order_qty = jnp.clip(2.0 * jax.random.uniform(arg_keys[0], (NX, SCEN), jnp.float32) ** steps_of(arg_keys[0], (NX, SCEN), ((0, 8), (1, 16)), -0.2, 0.2), 0.0, 2.0).astype(jnp.bfloat16)
    multiplier = scatter_about(arg_keys[1], (NX, SCEN), 1.0, 6.0, ((0, 8), (1, 16)), jnp.float32)
    unit_cost = scatter_about(arg_keys[2], (NX, SCEN), 1.0, 6.0, ((0, 8), (1, 16)))
    demand = scatter_about(arg_keys[3], (M, SCEN), 1.0, 6.0, ((0, 8), (1, 16)))
    technology = scatter_about(arg_keys[4], (NX, M), NX ** -0.5, 0.0625, ((0, 8),))
    kkt_inverse = draw_kkt_inverse(jax.random.fold_in(arg_keys[8], 71), 0)
    probability = jnp.clip(jnp.exp(math.log(1.0) - 2.3025851 * jax.random.uniform(arg_keys[6], (SCEN,), jnp.float32) ** steps_of(arg_keys[6], (SCEN,), ((0, 16),), -0.2, 0.2)), 0.1, 1.0)
    scenario_node = different_ones(arg_keys[7], SCEN, G, 1, 0)
    return {"order_qty": order_qty, "multiplier": multiplier, "unit_cost": unit_cost, "demand": demand, "technology": technology, "kkt_inverse": kkt_inverse, "probability": probability, "scenario_node": scenario_node}


step_size = 0.5
penalty = 2.0


def reference(order_qty, multiplier, unit_cost, demand, technology, kkt_inverse, probability, scenario_node):
    supply = jnp.dot(technology.T, order_qty, preferred_element_type=jnp.float32)
    right_side = (demand.astype(jnp.float32) - supply).astype(jnp.bfloat16)
    recourse = jnp.dot(kkt_inverse, right_side, preferred_element_type=jnp.float32).astype(jnp.bfloat16)
    gradient = unit_cost.astype(jnp.float32) + multiplier + jnp.dot(technology, recourse, preferred_element_type=jnp.float32)
    planned = jnp.maximum(order_qty.astype(jnp.float32) - step_size * gradient, 0.0).astype(jnp.bfloat16)
    nodes = scenario_node[:, 0].astype(jnp.int32)
    weighted = planned.astype(jnp.float32) * probability[None, :]
    totals = jax.ops.segment_sum(weighted.T, nodes, num_segments=G).T
    masses = jax.ops.segment_sum(probability, nodes, num_segments=G)
    consensus = totals / masses[None, :]
    multiplier_next = multiplier + penalty * (planned.astype(jnp.float32) - consensus[:, nodes])
    return planned, recourse, consensus, multiplier_next
```

```python
import jax
import jax.numpy as jnp
from jax import lax
from jax.experimental import pallas as pl
from jax.experimental.pallas import tpu as pltpu
from jax.sharding import PartitionSpec as P

G = 512
STEP = 0.5
PENALTY = 2.0

ROWS = 1024
S = 512
M = 2048
B = 256
HALF = 512
SLICE = 64

RA = 288
HA = RA // 2
RB = S - RA
HB = RB // 2

bf16 = jnp.bfloat16
f32 = jnp.float32
MESH = pl.DeviceIdType.MESH


def nt(a, b):
    return lax.dot_general(a, b, (((1,), (1,)), ((), ())), preferred_element_type=f32)


def nn(a, b):
    return jnp.dot(a, b, preferred_element_type=f32)


def kernel(
    order_hbm, mult_hbm, cost_hbm, demand_hbm, tech_hbm, kkt_hbm, prob_ref, node_ref,
    planned_out, recourse_out, cons_out, next_out,
    order_v, order_t, mult_v, cost_v, demand_v, tech_v, kkt_v,
    part,
    a1_s, a1_r, a2_s, a2_r, a3_s, a3_r,
    b1_s, b1_r, b2_s, b2_r, b3_s, b3_r,
    rhs, rec, rec_own,
    weight, member, mass_s, mass_r, mass_c, mass_p,
    planned_v, tot, e1_s, e1_r, e2_s, e2_r, cons_b, cons_f,
    load, tload, out_sem,
    rs_send, rs_recv, ag1_send, ag1_recv, ag2_send, ag2_recv,
    m_send, m_recv, e1_send, e1_recv, e2_send, e2_recv, f_send, f_recv, c_send, c_recv,
):
    s = lax.axis_index("scen")
    d = lax.axis_index("dec")
    x, y = d % 4, d // 4
    core, z, yh = s % 2, (s // 2) % 4, s // 8

    def dec_id(dx, dy):
        return ((y + dy) % 2) * 4 + (x + dx) % 4

    def peer_id(oy, oz):
        return ((yh + oy) % 2) * 4 + (z + oz) % 4

    right, left, across = (s, dec_id(1, 0)), (s, dec_id(3, 0)), (s, dec_id(0, 1))
    twin = (s - core + (1 - core), d)
    offsets = [(1, 0), (0, 2), (1, 2), (0, 1), (0, 3), (1, 1), (1, 3)]

    def peer(oy, oz):
        p = peer_id(oy, oz)
        return (p * 2 + core, d)

    barrier = pltpu.get_barrier_semaphore()
    everyone = [right, left, across, twin] + [peer(oy, oz) for oy, oz in offsets]
    for other in everyone:
        pl.semaphore_signal(barrier, inc=1, device_id=other, device_id_type=MESH)

    started = []

    def send(src, dst, ssem, rsem, k, target):
        copy = pltpu.make_async_remote_copy(
            src_ref=src, dst_ref=dst, send_sem=ssem.at[k], recv_sem=rsem.at[k],
            device_id=target, device_id_type=MESH,
        )
        copy.start()
        started.append(copy)
        return copy

    load_order = pltpu.make_async_copy(order_hbm, order_v, load.at[0])
    load_order.start()

    def tech_copy(r):
        dy, dx = tech_at(r)
        cols = pl.ds(pl.multiple_of(dec_id(dx, dy) * B, B), B)
        return pltpu.make_async_copy(tech_hbm.at[:, cols], tech_v.at[:, cols], tload.at[r])

    def tech_at(r):
        if r < 2:
            return 1 - r, 2
        return (1 if r < 5 else 0), (1 - (r - 2) % 3) % 4

    for r in range(8):
        tech_copy(r).start()
    others = [
        pltpu.make_async_copy(demand_hbm, demand_v, load.at[1]),
        pltpu.make_async_copy(kkt_hbm, kkt_v, load.at[2]),
        pltpu.make_async_copy(mult_hbm, mult_v, load.at[3]),
        pltpu.make_async_copy(cost_hbm, cost_v, load.at[4]),
    ]
    for copy in others:
        copy.start()

    load_order.wait()
    order_t[...] = order_v[...].T

    def first_product(dy, dx):
        cols = pl.ds(pl.multiple_of(dec_id(dx, dy) * B, B), B)
        part[dy, dx] = nn(order_t[...], tech_v[:, cols])

    tech_copy(0).wait()
    tech_copy(1).wait()

    @pl.loop(0, 2)
    def _(i):
        first_product(1 - i, 2)

    for dy in range(2):
        a1_s[0, dy] = part[dy, 2, 0:HA].astype(bf16)
        a1_s[1, dy] = part[dy, 2, HA:RA].astype(bf16)
    b1_s[2] = part[1, 2, RA:S].astype(bf16)

    pl.semaphore_wait(barrier, len(everyone))

    a1 = [
        send(a1_s.at[0], a1_r.at[0], rs_send, rs_recv, 0, right),
        send(a1_s.at[1], a1_r.at[1], rs_send, rs_recv, 1, left),
    ]
    b1 = {2: send(b1_s.at[2], b1_r.at[2], rs_send, rs_recv, 2, across)}

    for r in range(2, 5):
        tech_copy(r).wait()

    @pl.loop(0, 3)
    def _(i):
        first_product(1, (5 - i) % 4)

    for k, dx in enumerate((1, 3, 0)):
        b1_s[dx] = part[1, dx, RA:S].astype(bf16)
        b1[dx] = send(b1_s.at[dx], b1_r.at[dx], rs_send, rs_recv, 3 + k, across)

    for r in range(5, 8):
        tech_copy(r).wait()

    @pl.loop(0, 3)
    def _(i):
        first_product(0, (5 - i) % 4)

    a1[0].wait_recv()
    a1[1].wait_recv()
    a2 = {}
    for dy in (1, 0):
        a2_s[0, dy, 0:HA] = (part[dy, 1, 0:HA] + a1_r[0, dy].astype(f32)).astype(bf16)
        a2_s[0, dy, HA:RA] = part[dy, 1, HA:RA].astype(bf16)
        a2[0, dy] = send(a2_s.at[0, dy], a2_r.at[0, dy], rs_send, rs_recv, 6 + dy, right)
        a2_s[1, dy, 0:HA] = part[dy, 3, 0:HA].astype(bf16)
        a2_s[1, dy, HA:RA] = (part[dy, 3, HA:RA] + a1_r[1, dy].astype(f32)).astype(bf16)
        a2[1, dy] = send(a2_s.at[1, dy], a2_r.at[1, dy], rs_send, rs_recv, 8 + dy, left)
        if dy == 1:
            b1[2].wait_recv()
            b2_s[0] = (part[0, 2, RA:RA + HB] + b1_r[2, 0:HB].astype(f32)).astype(bf16)
            b2_s[1] = (part[0, 2, RA + HB:S] + b1_r[2, HB:RB].astype(f32)).astype(bf16)
            b2 = [
                send(b2_s.at[0], b2_r.at[0], rs_send, rs_recv, 10, right),
                send(b2_s.at[1], b2_r.at[1], rs_send, rs_recv, 11, left),
            ]

    node_ids = lax.broadcasted_iota(jnp.int32, (G, S), 0)
    same = node_ids == node_ref[...]
    member[...] = jnp.where(same, 1.0, 0.0).astype(bf16)
    weight[...] = jnp.where(same, prob_ref[...], 0.0).astype(bf16)
    mass_s[...] = nt(jnp.ones((16, S), bf16), weight[...])[0:8]
    mass_twin = send(mass_s, mass_r, m_send, m_recv, 0, twin)
    for copy in others:
        copy.wait()

    b1[1].wait_recv()
    b2[0].wait_recv()
    b3_s[0, 0:HB] = (
        part[0, 1, RA:RA + HB] + b1_r[1, 0:HB].astype(f32) + b2_r[0].astype(f32)
    ).astype(bf16)
    b3_s[0, HB:RB] = (part[0, 1, RA + HB:S] + b1_r[1, HB:RB].astype(f32)).astype(bf16)
    b3 = [send(b3_s.at[0], b3_r.at[0], rs_send, rs_recv, 12, right)]
    b1[3].wait_recv()
    b2[1].wait_recv()
    b3_s[1, 0:HB] = (part[0, 3, RA:RA + HB] + b1_r[3, 0:HB].astype(f32)).astype(bf16)
    b3_s[1, HB:RB] = (
        part[0, 3, RA + HB:S] + b1_r[3, HB:RB].astype(f32) + b2_r[1].astype(f32)
    ).astype(bf16)
    b3.append(send(b3_s.at[1], b3_r.at[1], rs_send, rs_recv, 13, left))

    a2[0, 1].wait_recv()
    a2[1, 1].wait_recv()
    a3_s[...] = (
        part[1, 0, 0:RA] + a2_r[0, 1].astype(f32) + a2_r[1, 1].astype(f32)
    ).astype(bf16)
    a3 = send(a3_s, a3_r, rs_send, rs_recv, 14, across)

    mass_twin.wait_recv()
    mass_c[...] = mass_s[...] + mass_r[...]
    mass_copies = [
        send(mass_c, mass_p.at[k], m_send, m_recv, 1 + k, peer(oy, oz))
        for k, (oy, oz) in enumerate(offsets)
    ]

    demand_t = demand_v[...].T
    own = pl.ds(pl.multiple_of(d * B, B), B)
    b1[0].wait_recv()
    b3[0].wait_recv()
    b3[1].wait_recv()
    rhs[RA:S, own] = (
        demand_t[RA:S].astype(f32)
        - (
            part[0, 0, RA:S] + b1_r[0].astype(f32)
            + b3_r[0].astype(f32) + b3_r[1].astype(f32)
        )
    ).astype(bf16)

    low0, low1 = (0, HA), (HA, HA)
    low = (0, RA)
    high = (RA, RB)
    high0, high1 = (RA, HB), (RA + HB, HB)

    def gatherer(buf, ssem, rsem):
        def go(rows, dx, dy, target, k):
            cols = pl.ds(pl.multiple_of(dec_id(dx, dy) * B, B), B)
            where = buf.at[pl.ds(*rows), cols]
            return send(where, where, ssem, rsem, k, target)

        c = {}

        def start_high():
            c[0] = go(high, 0, 0, right, 0)
            c[1] = go(high, 0, 0, left, 1)
            c[2] = go(high, 0, 0, across, 2)

        def start_low():
            c[9] = go(low, 0, 0, across, 9)
            c[10] = go(low, 0, 0, right, 10)
            c[11] = go(low, 0, 0, left, 11)

        def first_turn():
            c[0].wait_recv()
            c[3] = go(high0, 3, 0, right, 3)
            c[5] = go(high, 3, 0, across, 5)
            c[1].wait_recv()
            c[4] = go(high1, 1, 0, left, 4)
            c[6] = go(high, 1, 0, across, 6)

        def rest():
            c[9].wait_recv()
            c[12] = go(low, 0, 1, right, 12)
            c[13] = go(low, 0, 1, left, 13)
            c[3].wait_recv()
            c[7] = go(high0, 2, 0, across, 7)
            c[4].wait_recv()
            c[8] = go(high1, 2, 0, across, 8)
            c[10].wait_recv()
            c[14] = go(low0, 3, 0, right, 14)
            c[11].wait_recv()
            c[15] = go(low1, 1, 0, left, 15)
            c[12].wait_recv()
            c[16] = go(low0, 3, 1, right, 16)
            c[13].wait_recv()
            c[17] = go(low1, 1, 1, left, 17)

        def end_high():
            for k in (2, 5, 6, 7, 8):
                c[k].wait_recv()

        def end_low():
            for k in (14, 15, 16, 17):
                c[k].wait_recv()

        return start_high, start_low, first_turn, rest, end_high, end_low

    high_1, low_1, turn_1, rest_1, end_high_1, end_low_1 = gatherer(rhs, ag1_send, ag1_recv)
    high_2, low_2, turn_2, rest_2, end_high_2, end_low_2 = gatherer(rec, ag2_send, ag2_recv)

    high_1()
    a2[0, 0].wait_recv()
    a2[1, 0].wait_recv()
    a3.wait_recv()
    rhs[0:RA, own] = (
        demand_t[0:RA].astype(f32)
        - (
            part[0, 0, 0:RA] + a2_r[0, 0].astype(f32)
            + a2_r[1, 0].astype(f32) + a3_r[...].astype(f32)
        )
    ).astype(bf16)
    low_1()
    turn_1()
    rest_1()
    end_high_1()
    rec[RA:S, own] = nt(rhs[RA:S], kkt_v[...]).astype(bf16)
    high_2()
    end_low_1()
    rec[0:RA, own] = nt(rhs[0:RA], kkt_v[...]).astype(bf16)
    low_2()
    rec_own[...] = nt(kkt_v[...], rhs[...]).astype(bf16)
    write_rec = pltpu.make_async_copy(rec_own, recourse_out, out_sem.at[0])
    write_rec.start()
    turn_2()
    rest_2()
    end_high_2()
    end_low_2()

    CH = 128

    def plan(rows):
        linked = nt(tech_v[rows, :], rec[...])
        gradient = cost_v[rows, :].astype(f32) + mult_v[rows, :] + linked
        planned = jnp.maximum(order_v[rows, :].astype(f32) - STEP * gradient, 0.0).astype(bf16)
        planned_v[rows, :] = planned
        return nt(planned, weight[...])

    def core_copy(j):
        rows = pl.ds(pl.multiple_of(j * CH, CH), CH)
        return pltpu.make_async_remote_copy(
            src_ref=e1_s.at[rows], dst_ref=e1_r.at[rows],
            send_sem=e1_send.at[j], recv_sem=e1_recv.at[j],
            device_id=twin, device_id_type=MESH,
        )

    @pl.loop(0, HALF // CH)
    def _(j):
        rows = pl.ds(pl.multiple_of((1 - core) * HALF + j * CH, CH), CH)
        e1_s[pl.ds(pl.multiple_of(j * CH, CH), CH), :] = plan(rows).astype(bf16)
        core_copy(j).start()

    @pl.loop(0, HALF // CH)
    def _(j):
        rows = pl.ds(pl.multiple_of(core * HALF + j * CH, CH), CH)
        here = pl.ds(pl.multiple_of(j * CH, CH), CH)
        mine = plan(rows)
        core_copy(j).wait_recv()
        total = mine + e1_r[here, :].astype(f32)
        tot[here, :] = total
        e2_s[here, :] = total.astype(bf16)

    def slice_of(p):
        return pl.ds(pl.multiple_of(p * SLICE, SLICE), SLICE)

    e2 = [
        send(e2_s.at[slice_of(peer_id(oy, oz))], e2_r.at[k], e2_send, e2_recv, k, peer(oy, oz))
        for k, (oy, oz) in enumerate(offsets)
    ]
    write_planned = pltpu.make_async_copy(planned_v, planned_out, out_sem.at[1])
    write_planned.start()
    me = peer_id(0, 0)
    mass = mass_c[...]
    for k in range(7):
        mass_copies[k].wait_recv()
        mass = mass + mass_p[k]
    total = tot[slice_of(me), :]
    for k in range(7):
        e2[k].wait_recv()
        total = total + e2_r[k].astype(f32)

    def cons_at(c, p):
        return pl.ds(pl.multiple_of(c * HALF + p * SLICE, SLICE), SLICE)

    mine = cons_at(core, me)
    cons_b[mine, :] = (total / mass[0:1, :]).astype(bf16)
    f = [
        send(cons_b.at[mine], cons_b.at[mine], f_send, f_recv, k, peer(oy, oz))
        for k, (oy, oz) in enumerate(offsets)
    ]
    c = [send(cons_b.at[mine], cons_b.at[mine], c_send, c_recv, 7, twin)]
    for k, (oy, oz) in enumerate(offsets):
        f[k].wait_recv()
        theirs = cons_at(core, peer_id(oy, 4 - oz))
        c.append(send(cons_b.at[theirs], cons_b.at[theirs], c_send, c_recv, k, twin))

    def finish(which):
        @pl.loop(0, HALF // CH)
        def _(j):
            rows = pl.ds(pl.multiple_of(which * HALF + j * CH, CH), CH)
            spread = nn(cons_b[rows, :], member[...])
            cons_f[rows, :] = cons_b[rows, :].astype(f32)
            mult_v[rows, :] = mult_v[rows, :] + PENALTY * (planned_v[rows, :].astype(f32) - spread)

        both = pl.ds(pl.multiple_of(which * HALF, HALF), HALF)
        return both

    writes = []

    def put(both, k):
        writes.append(pltpu.make_async_copy(cons_f.at[both], cons_out.at[both], out_sem.at[2 + k]))
        writes.append(pltpu.make_async_copy(mult_v.at[both], next_out.at[both], out_sem.at[4 + k]))
        writes[-1].start()
        writes[-2].start()

    put(finish(core), 0)
    for copy in c:
        copy.wait_recv()
    put(finish(1 - core), 1)

    for copy in started:
        copy.wait_send()
    for j in range(HALF // CH):
        core_copy(j).wait_send()
    write_rec.wait()
    write_planned.wait()
    for copy in writes:
        copy.wait()


def on_device(
    order_qty, multiplier, unit_cost, demand, technology, kkt_inverse, probability, scenario_node
):
    any_space = pl.BlockSpec(memory_space=pl.ANY)
    vmem = pl.BlockSpec(memory_space=pltpu.VMEM)
    V = pltpu.VMEM
    D = pltpu.SemaphoreType.DMA
    scratch = [
        V((ROWS, S), bf16), V((S, ROWS), bf16), V((ROWS, S), f32), V((ROWS, S), bf16),
        V((B, S), bf16), V((ROWS, M), bf16), V((B, M), bf16),
        V((2, 4, S, B), f32),
        V((2, 2, HA, B), bf16), V((2, 2, HA, B), bf16),
        V((2, 2, RA, B), bf16), V((2, 2, RA, B), bf16),
        V((RA, B), bf16), V((RA, B), bf16),
        V((4, RB, B), bf16), V((4, RB, B), bf16),
        V((2, HB, B), bf16), V((2, HB, B), bf16),
        V((2, RB, B), bf16), V((2, RB, B), bf16),
        V((S, M), bf16), V((S, M), bf16), V((B, S), bf16),
        V((G, S), bf16), V((G, S), bf16),
        V((8, G), f32), V((8, G), f32), V((8, G), f32), V((7, 8, G), f32),
        V((ROWS, S), bf16), V((HALF, G), f32), V((HALF, G), bf16), V((HALF, G), bf16),
        V((HALF, G), bf16), V((7, SLICE, G), bf16), V((ROWS, G), bf16), V((ROWS, G), f32),
        D((5,)), D((8,)), D((6,)),
        D((15,)), D((15,)), D((18,)), D((18,)), D((18,)), D((18,)),
        D((8,)), D((8,)), D((4,)), D((4,)), D((7,)), D((7,)), D((7,)), D((7,)), D((8,)), D((8,)),
    ]
    return tuple(
        pl.pallas_call(
            kernel,
            out_shape=(
                jax.ShapeDtypeStruct((ROWS, S), bf16),
                jax.ShapeDtypeStruct((B, S), bf16),
                jax.ShapeDtypeStruct((ROWS, G), f32),
                jax.ShapeDtypeStruct((ROWS, S), f32),
            ),
            in_specs=[any_space] * 6 + [vmem] * 2,
            out_specs=(any_space,) * 4,
            scratch_shapes=scratch,
            compiler_params=pltpu.CompilerParams(
                collective_id=0, has_side_effects=True, vmem_limit_bytes=56 * 2**20
            ),
        )(
            order_qty, multiplier, unit_cost, demand, technology, kkt_inverse,
            probability.reshape(1, S), scenario_node.reshape(1, S),
        )
    )


def solution(mesh):
    placed = (
        P("dec", "scen"),
        P("dec", "scen"),
        P("dec", "scen"),
        P("dec", "scen"),
        P("dec", None),
        P("dec", None),
        P("scen"),
        P("scen", None),
    )
    return jax.shard_map(
        on_device,
        mesh=mesh,
        in_specs=placed,
        out_specs=(P("dec", "scen"), P("dec", "scen"), P("dec", None), P("dec", "scen")),
        check_vma=False,
    )
```

```python
import jax
import jax.numpy as jnp
from jax import lax
from jax.experimental import pallas as pl
from jax.experimental.pallas import tpu as pltpu
from jax.sharding import PartitionSpec as P

G = 512
STEP = 0.5
PENALTY = 2.0

ROWS = 1024
S = 512
M = 2048
B = 256
SLICE = 64
CH = 256

RA = 288
HA = RA // 2
RB = S - RA
HB = RB // 2

bf16 = jnp.bfloat16
f32 = jnp.float32
MESH = pl.DeviceIdType.MESH


def nt(a, b):
    return lax.dot_general(a, b, (((1,), (1,)), ((), ())), preferred_element_type=f32)


def nn(a, b):
    return jnp.dot(a, b, preferred_element_type=f32)


def kernel(
    order_hbm, mult_hbm, cost_hbm, demand_hbm, tech_hbm, kkt_hbm, prob_ref, node_ref,
    planned_out, recourse_out, cons_out,
    order_v, order_t, mult_v, cost_v, demand_v, tech_v, kkt_v,
    part,
    a1_s, a1_r, a2_s, a2_r, a3_s, a3_r,
    b1_s, b1_r, b2_s, b2_r, b3_s, b3_r,
    rhs, rec, rec_own,
    weight, mass_s, mass_r,
    planned_v, tot, e1_s, e1_r, e2_s, e2_r, cons_b,
    load, tload, out_sem,
    rs_send, rs_recv, ag1_send, ag1_recv, ag2_send, ag2_recv,
    m_send, m_recv, e1_send, e1_recv, e2_send, e2_recv, f_send, f_recv, c_send, c_recv,
):
    s = lax.axis_index("scen")
    d = lax.axis_index("dec")
    x, y = d % 4, d // 4
    core, z, yh = s % 2, (s // 2) % 4, s // 8

    def dec_id(dx, dy):
        return ((y + dy) % 2) * 4 + (x + dx) % 4

    def peer_id(oy, oz):
        return ((yh + oy) % 2) * 4 + (z + oz) % 4

    right, left, across = (s, dec_id(1, 0)), (s, dec_id(3, 0)), (s, dec_id(0, 1))
    twin = (s - core + (1 - core), d)
    offsets = [(1, 2), (0, 2), (1, 1), (1, 3), (1, 0), (0, 1), (0, 3)]

    def peer(oy, oz):
        p = peer_id(oy, oz)
        return (p * 2 + core, d)

    up, down, over = peer(0, 1), peer(0, 3), peer(1, 0)

    barrier = pltpu.get_barrier_semaphore()
    everyone = [right, left, across, twin, up, down, over]
    for other in everyone:
        pl.semaphore_signal(barrier, inc=1, device_id=other, device_id_type=MESH)

    started = []

    def send(src, dst, ssem, rsem, k, target):
        copy = pltpu.make_async_remote_copy(
            src_ref=src, dst_ref=dst, send_sem=ssem.at[k], recv_sem=rsem.at[k],
            device_id=target, device_id_type=MESH,
        )
        copy.start()
        started.append(copy)
        return copy

    load_order = pltpu.make_async_copy(order_hbm, order_v, load.at[0])
    load_order.start()

    def tech_copy(r):
        dy, dx = tech_at(r)
        cols = pl.ds(pl.multiple_of(dec_id(dx, dy) * B, B), B)
        return pltpu.make_async_copy(tech_hbm.at[:, cols], tech_v.at[:, cols], tload.at[r])

    def tech_at(r):
        if r < 2:
            return 1 - r, 2
        return (1 if r < 5 else 0), (1 - (r - 2) % 3) % 4

    for r in range(8):
        tech_copy(r).start()
    others = [
        pltpu.make_async_copy(demand_hbm, demand_v, load.at[1]),
        pltpu.make_async_copy(kkt_hbm, kkt_v, load.at[2]),
        pltpu.make_async_copy(mult_hbm, mult_v, load.at[3]),
        pltpu.make_async_copy(cost_hbm, cost_v, load.at[4]),
    ]
    for copy in others:
        copy.start()

    load_order.wait()
    order_t[...] = order_v[...].T

    def first_product(dy, dx):
        cols = pl.ds(pl.multiple_of(dec_id(dx, dy) * B, B), B)
        part[dy, dx] = nn(order_t[...], tech_v[:, cols])

    tech_copy(0).wait()
    tech_copy(1).wait()

    @pl.loop(0, 2)
    def _(i):
        first_product(1 - i, 2)

    for dy in range(2):
        a1_s[0, dy] = part[dy, 2, 0:HA].astype(bf16)
        a1_s[1, dy] = part[dy, 2, HA:RA].astype(bf16)
    b1_s[2] = part[1, 2, RA:S].astype(bf16)

    pl.semaphore_wait(barrier, len(everyone))

    a1 = [
        send(a1_s.at[0], a1_r.at[0], rs_send, rs_recv, 0, right),
        send(a1_s.at[1], a1_r.at[1], rs_send, rs_recv, 1, left),
    ]
    b1 = {2: send(b1_s.at[2], b1_r.at[2], rs_send, rs_recv, 2, across)}

    for r in range(2, 5):
        tech_copy(r).wait()

    @pl.loop(0, 3)
    def _(i):
        first_product(1, (5 - i) % 4)

    for k, dx in enumerate((1, 3, 0)):
        b1_s[dx] = part[1, dx, RA:S].astype(bf16)
        b1[dx] = send(b1_s.at[dx], b1_r.at[dx], rs_send, rs_recv, 3 + k, across)

    for r in range(5, 8):
        tech_copy(r).wait()

    @pl.loop(0, 3)
    def _(i):
        first_product(0, (5 - i) % 4)

    node_ids = lax.broadcasted_iota(jnp.int32, (G, S), 0)
    weight[...] = jnp.where(node_ids == node_ref[...], prob_ref[...], 0.0).astype(bf16)
    mass_s[0] = nt(jnp.ones((16, S), bf16), weight[...])[0:8]
    mass_twin = send(mass_s.at[0], mass_r.at[0], m_send, m_recv, 0, twin)

    a1[0].wait_recv()
    a1[1].wait_recv()
    a2 = {}
    for dy in (1, 0):
        a2_s[0, dy, 0:HA] = (part[dy, 1, 0:HA] + a1_r[0, dy].astype(f32)).astype(bf16)
        a2_s[0, dy, HA:RA] = part[dy, 1, HA:RA].astype(bf16)
        a2[0, dy] = send(a2_s.at[0, dy], a2_r.at[0, dy], rs_send, rs_recv, 6 + dy, right)
        a2_s[1, dy, 0:HA] = part[dy, 3, 0:HA].astype(bf16)
        a2_s[1, dy, HA:RA] = (part[dy, 3, HA:RA] + a1_r[1, dy].astype(f32)).astype(bf16)
        a2[1, dy] = send(a2_s.at[1, dy], a2_r.at[1, dy], rs_send, rs_recv, 8 + dy, left)
        if dy == 1:
            b1[2].wait_recv()
            b2_s[0] = (part[0, 2, RA:RA + HB] + b1_r[2, 0:HB].astype(f32)).astype(bf16)
            b2_s[1] = (part[0, 2, RA + HB:S] + b1_r[2, HB:RB].astype(f32)).astype(bf16)
            b2 = [
                send(b2_s.at[0], b2_r.at[0], rs_send, rs_recv, 10, right),
                send(b2_s.at[1], b2_r.at[1], rs_send, rs_recv, 11, left),
            ]

    mass_twin.wait_recv()
    mass_s[1] = mass_s[0] + mass_r[0]
    mass_over = send(mass_s.at[1], mass_r.at[1], m_send, m_recv, 1, over)
    for copy in others:
        copy.wait()

    b1[1].wait_recv()
    b2[0].wait_recv()
    b3_s[0, 0:HB] = (
        part[0, 1, RA:RA + HB] + b1_r[1, 0:HB].astype(f32) + b2_r[0].astype(f32)
    ).astype(bf16)
    b3_s[0, HB:RB] = (part[0, 1, RA + HB:S] + b1_r[1, HB:RB].astype(f32)).astype(bf16)
    b3 = [send(b3_s.at[0], b3_r.at[0], rs_send, rs_recv, 12, right)]
    b1[3].wait_recv()
    b2[1].wait_recv()
    b3_s[1, 0:HB] = (part[0, 3, RA:RA + HB] + b1_r[3, 0:HB].astype(f32)).astype(bf16)
    b3_s[1, HB:RB] = (
        part[0, 3, RA + HB:S] + b1_r[3, HB:RB].astype(f32) + b2_r[1].astype(f32)
    ).astype(bf16)
    b3.append(send(b3_s.at[1], b3_r.at[1], rs_send, rs_recv, 13, left))

    a2[0, 1].wait_recv()
    a2[1, 1].wait_recv()
    a3_s[...] = (
        part[1, 0, 0:RA] + a2_r[0, 1].astype(f32) + a2_r[1, 1].astype(f32)
    ).astype(bf16)
    a3 = send(a3_s, a3_r, rs_send, rs_recv, 14, across)

    mass_over.wait_recv()
    mass_s[2] = mass_s[1] + mass_r[1]
    mass_z = [
        send(mass_s.at[2], mass_r.at[2], m_send, m_recv, 2, up),
        send(mass_s.at[2], mass_r.at[3], m_send, m_recv, 3, down),
    ]

    demand_t = demand_v[...].T
    own = pl.ds(pl.multiple_of(d * B, B), B)
    b1[0].wait_recv()
    b3[0].wait_recv()
    b3[1].wait_recv()
    rhs[RA:S, own] = (
        demand_t[RA:S].astype(f32)
        - (
            part[0, 0, RA:S] + b1_r[0].astype(f32)
            + b3_r[0].astype(f32) + b3_r[1].astype(f32)
        )
    ).astype(bf16)

    low0, low1 = (0, HA), (HA, HA)
    low = (0, RA)
    high = (RA, RB)
    high0, high1 = (RA, HB), (RA + HB, HB)

    def gatherer(buf, ssem, rsem):
        def go(rows, dx, dy, target, k):
            cols = pl.ds(pl.multiple_of(dec_id(dx, dy) * B, B), B)
            where = buf.at[pl.ds(*rows), cols]
            return send(where, where, ssem, rsem, k, target)

        c = {}

        def start_high():
            c[0] = go(high, 0, 0, right, 0)
            c[1] = go(high, 0, 0, left, 1)
            c[2] = go(high, 0, 0, across, 2)

        def start_low():
            c[9] = go(low, 0, 0, across, 9)
            c[10] = go(low, 0, 0, right, 10)
            c[11] = go(low, 0, 0, left, 11)

        def first_turn():
            c[0].wait_recv()
            c[3] = go(high0, 3, 0, right, 3)
            c[5] = go(high, 3, 0, across, 5)
            c[1].wait_recv()
            c[4] = go(high1, 1, 0, left, 4)
            c[6] = go(high, 1, 0, across, 6)

        def rest():
            c[9].wait_recv()
            c[12] = go(low, 0, 1, right, 12)
            c[13] = go(low, 0, 1, left, 13)
            c[3].wait_recv()
            c[7] = go(high0, 2, 0, across, 7)
            c[4].wait_recv()
            c[8] = go(high1, 2, 0, across, 8)
            c[10].wait_recv()
            c[14] = go(low0, 3, 0, right, 14)
            c[11].wait_recv()
            c[15] = go(low1, 1, 0, left, 15)
            c[12].wait_recv()
            c[16] = go(low0, 3, 1, right, 16)
            c[13].wait_recv()
            c[17] = go(low1, 1, 1, left, 17)

        def end_high():
            for k in (2, 5, 6, 7, 8):
                c[k].wait_recv()

        def end_low():
            for k in (14, 15, 16, 17):
                c[k].wait_recv()

        return start_high, start_low, first_turn, rest, end_high, end_low

    high_1, low_1, turn_1, rest_1, end_high_1, end_low_1 = gatherer(rhs, ag1_send, ag1_recv)
    high_2, low_2, turn_2, rest_2, end_high_2, end_low_2 = gatherer(rec, ag2_send, ag2_recv)

    high_1()
    a2[0, 0].wait_recv()
    a2[1, 0].wait_recv()
    a3.wait_recv()
    rhs[0:RA, own] = (
        demand_t[0:RA].astype(f32)
        - (
            part[0, 0, 0:RA] + a2_r[0, 0].astype(f32)
            + a2_r[1, 0].astype(f32) + a3_r[...].astype(f32)
        )
    ).astype(bf16)
    low_1()
    turn_1()
    rest_1()
    end_high_1()
    rec[RA:S, own] = nt(rhs[RA:S], kkt_v[...]).astype(bf16)
    high_2()
    end_low_1()
    rec[0:RA, own] = nt(rhs[0:RA], kkt_v[...]).astype(bf16)
    low_2()
    rec_own[...] = nt(kkt_v[...], rhs[...]).astype(bf16)
    write_rec = pltpu.make_async_copy(rec_own, recourse_out, out_sem.at[0])
    write_rec.start()
    mass_z[0].wait_recv()
    mass_z[1].wait_recv()
    mass_z.append(send(mass_s.at[2], mass_r.at[4], m_send, m_recv, 4, peer(0, 2)))
    turn_2()
    rest_2()
    end_high_2()
    end_low_2()

    def plan(rows):
        linked = nt(tech_v[rows, :], rec[...])
        gradient = cost_v[rows, :].astype(f32) + mult_v[rows, :] + linked
        planned = jnp.maximum(order_v[rows, :].astype(f32) - STEP * gradient, 0.0).astype(bf16)
        planned_v[rows, :] = planned
        return nt(planned, weight[...])

    def core_copy(j):
        return pltpu.make_async_remote_copy(
            src_ref=e1_s.at[j], dst_ref=e1_r.at[j],
            send_sem=e1_send.at[j], recv_sem=e1_recv.at[j],
            device_id=twin, device_id_type=MESH,
        )

    def slice_copy(oy, oz):
        k = oz * 2 + oy
        rows = pl.ds(pl.multiple_of(((yh + oy) % 2) * SLICE, SLICE), SLICE)
        return pltpu.make_async_remote_copy(
            src_ref=e2_s.at[oz, rows], dst_ref=e2_r.at[k],
            send_sem=e2_send.at[k], recv_sem=e2_recv.at[k],
            device_id=peer(oy, oz), device_id_type=MESH,
        )

    def core_rows(c):
        return pl.ds(pl.multiple_of(c * (CH // 2), CH // 2), CH // 2)

    def join(oz):
        core_copy(oz).wait_recv()
        total = tot[oz, core_rows(core), :] + e1_r[oz].astype(f32)
        tot[oz, core_rows(core), :] = total
        e2_s[oz] = total.astype(bf16)

    def compute(oz):
        tot[oz] = plan(pl.ds(pl.multiple_of(((z + oz) % 4) * CH, CH), CH))
        e1_s[oz] = tot[oz, core_rows(1 - core), :].astype(bf16)
        core_copy(oz).start()

    compute(3)

    @pl.loop(0, 3)
    def _(j):
        compute(2 - j)
        join(3 - j)
        slice_copy(0, 3 - j).start()
        slice_copy(1, 3 - j).start()

    join(0)
    slice_copy(1, 0).start()
    write_planned = pltpu.make_async_copy(planned_v, planned_out, out_sem.at[1])
    write_planned.start()
    mass_z[2].wait_recv()
    mass = mass_s[2] + mass_r[2] + mass_r[3] + mass_r[4]
    total = tot[0, pl.ds(pl.multiple_of(core * (CH // 2) + yh * SLICE, SLICE), SLICE), :]
    for oy, oz in ((0, 3), (1, 3), (0, 2), (1, 2), (0, 1), (1, 1), (1, 0)):
        slice_copy(oy, oz).wait_recv()
        total = total + e2_r[oz * 2 + oy].astype(f32)

    def cons_at(oy, oz):
        first = ((z + oz) % 4) * CH + core * (CH // 2) + ((yh + oy) % 2) * SLICE
        return pl.ds(pl.multiple_of(first, SLICE), SLICE)

    mine = cons_at(0, 0)
    cons_b[mine, :] = (total / mass[0:1, :]).astype(bf16)
    f = [
        send(cons_b.at[mine], cons_b.at[mine], f_send, f_recv, k, peer(oy, oz))
        for k, (oy, oz) in enumerate(offsets)
    ]
    c = [send(cons_b.at[mine], cons_b.at[mine], c_send, c_recv, 7, twin)]
    for k, (oy, oz) in reversed(list(enumerate(offsets))):
        f[k].wait_recv()
        theirs = cons_at(oy, 4 - oz)
        c.append(send(cons_b.at[theirs], cons_b.at[theirs], c_send, c_recv, k, twin))
    for copy in c:
        copy.wait_recv()
    write_cons = pltpu.make_async_copy(cons_b, cons_out, out_sem.at[2])
    write_cons.start()

    for copy in started:
        copy.wait_send()
    for oz in range(4):
        core_copy(oz).wait_send()
        for oy in range(2):
            if oz or oy:
                slice_copy(oy, oz).wait_send()
    write_rec.wait()
    write_planned.wait()
    write_cons.wait()


def last_kernel(
    planned_hbm, recourse_hbm, cons_hbm, mult_hbm, node_ref,
    planned_out, recourse_out, cons_out, next_out,
    planned_v, recourse_v, cons_v, mult_v, cons_f, member, load, out_sem,
):
    pairs = ((planned_hbm, planned_v), (recourse_hbm, recourse_v), (cons_hbm, cons_v))
    loads = [pltpu.make_async_copy(a, b, load.at[k]) for k, (a, b) in enumerate(pairs)]
    loads.append(pltpu.make_async_copy(mult_hbm, mult_v, load.at[3]))
    for copy in loads:
        copy.start()
    node_ids = lax.broadcasted_iota(jnp.int32, (G, S), 0)
    member[...] = jnp.where(node_ids == node_ref[...], 1.0, 0.0).astype(bf16)
    loads[0].wait()
    writes = [pltpu.make_async_copy(planned_v, planned_out, out_sem.at[0])]
    writes[0].start()
    loads[1].wait()
    writes.append(pltpu.make_async_copy(recourse_v, recourse_out, out_sem.at[1]))
    writes[1].start()
    loads[2].wait()
    loads[3].wait()

    def put(j):
        rows = pl.ds(pl.multiple_of(j * CH, CH), CH)
        return (
            pltpu.make_async_copy(cons_f.at[rows], cons_out.at[rows], out_sem.at[2 + j]),
            pltpu.make_async_copy(mult_v.at[rows], next_out.at[rows], out_sem.at[6 + j]),
        )

    @pl.loop(0, ROWS // CH)
    def _(j):
        rows = pl.ds(pl.multiple_of(j * CH, CH), CH)
        spread = nn(cons_v[rows, :], member[...])
        cons_f[rows, :] = cons_v[rows, :].astype(f32)
        mult_v[rows, :] = mult_v[rows, :] + PENALTY * (planned_v[rows, :].astype(f32) - spread)
        for copy in put(j):
            copy.start()

    for copy in writes:
        copy.wait()
    for j in range(ROWS // CH):
        for copy in put(j):
            copy.wait()


def on_device(
    order_qty, multiplier, unit_cost, demand, technology, kkt_inverse, probability, scenario_node
):
    any_space = pl.BlockSpec(memory_space=pl.ANY)
    vmem = pl.BlockSpec(memory_space=pltpu.VMEM)
    hbm = pl.BlockSpec(memory_space=pltpu.HBM)
    V = pltpu.VMEM
    D = pltpu.SemaphoreType.DMA
    scratch = [
        V((ROWS, S), bf16), V((S, ROWS), bf16), V((ROWS, S), f32), V((ROWS, S), bf16),
        V((B, S), bf16), V((ROWS, M), bf16), V((B, M), bf16),
        V((2, 4, S, B), f32),
        V((2, 2, HA, B), bf16), V((2, 2, HA, B), bf16),
        V((2, 2, RA, B), bf16), V((2, 2, RA, B), bf16),
        V((RA, B), bf16), V((RA, B), bf16),
        V((4, RB, B), bf16), V((4, RB, B), bf16),
        V((2, HB, B), bf16), V((2, HB, B), bf16),
        V((2, RB, B), bf16), V((2, RB, B), bf16),
        V((S, M), bf16), V((S, M), bf16), V((B, S), bf16),
        V((G, S), bf16), V((3, 8, G), f32), V((5, 8, G), f32),
        V((ROWS, S), bf16), V((4, CH, G), f32),
        V((4, CH // 2, G), bf16), V((4, CH // 2, G), bf16),
        V((4, CH // 2, G), bf16), V((8, SLICE, G), bf16), V((ROWS, G), bf16),
        D((5,)), D((8,)), D((3,)),
        D((15,)), D((15,)), D((18,)), D((18,)), D((18,)), D((18,)),
        D((5,)), D((5,)), D((4,)), D((4,)), D((8,)), D((8,)), D((7,)), D((7,)), D((8,)), D((8,)),
    ]
    node_row = scenario_node.reshape(1, S)
    planned, recourse, consensus = pl.pallas_call(
        kernel,
        out_shape=(
            jax.ShapeDtypeStruct((ROWS, S), bf16),
            jax.ShapeDtypeStruct((B, S), bf16),
            jax.ShapeDtypeStruct((ROWS, G), bf16),
        ),
        in_specs=[any_space] * 6 + [vmem] * 2,
        out_specs=(any_space,) * 3,
        scratch_shapes=scratch,
        compiler_params=pltpu.CompilerParams(
            collective_id=0, has_side_effects=True, vmem_limit_bytes=56 * 2**20
        ),
    )(
        order_qty, multiplier, unit_cost, demand, technology, kkt_inverse,
        probability.reshape(1, S), node_row,
    )
    return tuple(
        pl.pallas_call(
            last_kernel,
            out_shape=(
                jax.ShapeDtypeStruct((ROWS, S), bf16),
                jax.ShapeDtypeStruct((B, S), bf16),
                jax.ShapeDtypeStruct((ROWS, G), f32),
                jax.ShapeDtypeStruct((ROWS, S), f32),
            ),
            in_specs=[hbm] * 4 + [vmem],
            out_specs=(any_space,) * 4,
            scratch_shapes=[
                V((ROWS, S), bf16), V((B, S), bf16), V((ROWS, G), bf16), V((ROWS, S), f32),
                V((ROWS, G), f32), V((G, S), bf16), D((4,)), D((10,)),
            ],
            compiler_params=pltpu.CompilerParams(vmem_limit_bytes=32 * 2**20),
        )(planned, recourse, consensus, multiplier, node_row)
    )


def solution(mesh):
    placed = (
        P("dec", "scen"),
        P("dec", "scen"),
        P("dec", "scen"),
        P("dec", "scen"),
        P("dec", None),
        P("dec", None),
        P("scen"),
        P("scen", None),
    )
    return jax.shard_map(
        on_device,
        mesh=mesh,
        in_specs=placed,
        out_specs=(P("dec", "scen"), P("dec", "scen"), P("dec", None), P("dec", "scen")),
        check_vma=False,
    )
```

```python
import jax
import jax.numpy as jnp
from jax import lax
from jax.experimental import pallas as pl
from jax.experimental.pallas import tpu as pltpu
from jax.sharding import PartitionSpec as P

G = 512
STEP = 0.5
PENALTY = 2.0

ROWS = 1024
S = 512
M = 2048
B = 256
SLICE = 64
CH = 256
PIECE = M // 16

RA = 288
HA = RA // 2
RB = S - RA
HB = RB // 2

bf16 = jnp.bfloat16
f32 = jnp.float32
MESH = pl.DeviceIdType.MESH


def nt(a, b):
    return lax.dot_general(a, b, (((1,), (1,)), ((), ())), preferred_element_type=f32)


def nn(a, b):
    return jnp.dot(a, b, preferred_element_type=f32)


def kernel(
    order_hbm, mult_hbm, cost_hbm, demand_hbm, tech_hbm, kkt_hbm, prob_ref, node_ref,
    planned_out, recourse_out, cons_out,
    order_v, order_t, mult_v, cost_v, demand_v, tech_v, kkt_v,
    part,
    a1_s, a1_r, a2_s, a2_r, a3_s, a3_r,
    b1_s, b1_r, b2_s, b2_r, b3_s, b3_r,
    rhs, link, kkt_cols, rec_own,
    weight, mass_s, mass_r,
    planned_v, tot, e1_s, e1_r, e2_s, e2_r, cons_b,
    load, tload, out_sem,
    rs_send, rs_recv, ag1_send, ag1_recv, k_send, k_recv, l_send, l_recv, t_send, t_recv,
    m_send, m_recv, e1_send, e1_recv, e2_send, e2_recv, f_send, f_recv, c_send, c_recv,
):
    s = lax.axis_index("scen")
    d = lax.axis_index("dec")
    x, y = d % 4, d // 4
    core, z, yh = s % 2, (s // 2) % 4, s // 8

    def dec_id(dx, dy):
        return ((y + dy) % 2) * 4 + (x + dx) % 4

    def peer_id(oy, oz):
        return ((yh + oy) % 2) * 4 + (z + oz) % 4

    right, left, across = (s, dec_id(1, 0)), (s, dec_id(3, 0)), (s, dec_id(0, 1))
    twin = (s - core + (1 - core), d)
    offsets = [(1, 2), (0, 2), (1, 1), (1, 3), (1, 0), (0, 1), (0, 3)]

    def peer(oy, oz):
        p = peer_id(oy, oz)
        return (p * 2 + core, d)

    up, down, over = peer(0, 1), peer(0, 3), peer(1, 0)

    barrier = pltpu.get_barrier_semaphore()
    everyone = [right, left, across, twin, up, down, over]
    for other in everyone:
        pl.semaphore_signal(barrier, inc=1, device_id=other, device_id_type=MESH)

    started = []

    def send(src, dst, ssem, rsem, k, target):
        copy = pltpu.make_async_remote_copy(
            src_ref=src, dst_ref=dst, send_sem=ssem.at[k], recv_sem=rsem.at[k],
            device_id=target, device_id_type=MESH,
        )
        copy.start()
        started.append(copy)
        return copy

    piece = pl.ds(pl.multiple_of(s * PIECE, PIECE), PIECE)
    kkt_rows = pl.ds(pl.multiple_of(d * B, B), B)
    load_piece = pltpu.make_async_copy(
        kkt_hbm.at[:, piece], kkt_cols.at[kkt_rows, :], load.at[5]
    )
    load_piece.start()
    load_order = pltpu.make_async_copy(order_hbm, order_v, load.at[0])
    load_order.start()

    def tech_copy(r):
        dy, dx = tech_at(r)
        cols = pl.ds(pl.multiple_of(dec_id(dx, dy) * B, B), B)
        return pltpu.make_async_copy(tech_hbm.at[:, cols], tech_v.at[:, cols], tload.at[r])

    def tech_at(r):
        if r < 2:
            return 1 - r, 2
        return (1 if r < 5 else 0), (1 - (r - 2) % 3) % 4

    for r in range(8):
        tech_copy(r).start()
    others = [
        pltpu.make_async_copy(demand_hbm, demand_v, load.at[1]),
        pltpu.make_async_copy(kkt_hbm, kkt_v, load.at[2]),
        pltpu.make_async_copy(mult_hbm, mult_v, load.at[3]),
        pltpu.make_async_copy(cost_hbm, cost_v, load.at[4]),
    ]
    for copy in others:
        copy.start()

    load_order.wait()
    order_t[...] = order_v[...].T

    def first_product(dy, dx):
        cols = pl.ds(pl.multiple_of(dec_id(dx, dy) * B, B), B)
        part[dy, dx] = nn(order_t[...], tech_v[:, cols])

    tech_copy(0).wait()
    tech_copy(1).wait()

    @pl.loop(0, 2)
    def _(i):
        first_product(1 - i, 2)

    for dy in range(2):
        a1_s[0, dy] = part[dy, 2, 0:HA].astype(bf16)
        a1_s[1, dy] = part[dy, 2, HA:RA].astype(bf16)
    b1_s[2] = part[1, 2, RA:S].astype(bf16)

    pl.semaphore_wait(barrier, len(everyone))

    def kkt_send(dx, dy, part_of, target, k):
        first, size = part_of
        e = pl.ds(pl.multiple_of(dec_id(dx, dy) * B + first, B // 2), size)
        return send(kkt_cols.at[e, :], kkt_cols.at[e, :], k_send, k_recv, k, target)

    whole, half0, half1 = (0, B), (0, B // 2), (B // 2, B // 2)
    load_piece.wait()
    kc = [
        kkt_send(0, 0, whole, across, 0),
        kkt_send(0, 0, whole, right, 1),
        kkt_send(0, 0, whole, left, 2),
    ]
    a1 = [
        send(a1_s.at[0], a1_r.at[0], rs_send, rs_recv, 0, right),
        send(a1_s.at[1], a1_r.at[1], rs_send, rs_recv, 1, left),
    ]
    b1 = {2: send(b1_s.at[2], b1_r.at[2], rs_send, rs_recv, 2, across)}

    for r in range(2, 5):
        tech_copy(r).wait()

    @pl.loop(0, 3)
    def _(i):
        first_product(1, (5 - i) % 4)

    for k, dx in enumerate((1, 3, 0)):
        b1_s[dx] = part[1, dx, RA:S].astype(bf16)
        b1[dx] = send(b1_s.at[dx], b1_r.at[dx], rs_send, rs_recv, 3 + k, across)

    for r in range(5, 8):
        tech_copy(r).wait()
    kc[0].wait_recv()
    kc.append(kkt_send(0, 1, whole, right, 3))
    kc.append(kkt_send(0, 1, whole, left, 4))

    @pl.loop(0, 3)
    def _(i):
        first_product(0, (5 - i) % 4)

    kc[1].wait_recv()
    kc.append(kkt_send(3, 0, half0, right, 5))
    kc[2].wait_recv()
    kc.append(kkt_send(1, 0, half1, left, 6))

    node_ids = lax.broadcasted_iota(jnp.int32, (G, S), 0)
    weight[...] = jnp.where(node_ids == node_ref[...], prob_ref[...], 0.0).astype(bf16)
    mass_s[0] = nt(jnp.ones((16, S), bf16), weight[...])[0:8]
    mass_twin = send(mass_s.at[0], mass_r.at[0], m_send, m_recv, 0, twin)

    a1[0].wait_recv()
    a1[1].wait_recv()
    a2 = {}
    for dy in (1, 0):
        a2_s[0, dy, 0:HA] = (part[dy, 1, 0:HA] + a1_r[0, dy].astype(f32)).astype(bf16)
        a2_s[0, dy, HA:RA] = part[dy, 1, HA:RA].astype(bf16)
        a2[0, dy] = send(a2_s.at[0, dy], a2_r.at[0, dy], rs_send, rs_recv, 6 + dy, right)
        a2_s[1, dy, 0:HA] = part[dy, 3, 0:HA].astype(bf16)
        a2_s[1, dy, HA:RA] = (part[dy, 3, HA:RA] + a1_r[1, dy].astype(f32)).astype(bf16)
        a2[1, dy] = send(a2_s.at[1, dy], a2_r.at[1, dy], rs_send, rs_recv, 8 + dy, left)
        if dy == 1:
            b1[2].wait_recv()
            b2_s[0] = (part[0, 2, RA:RA + HB] + b1_r[2, 0:HB].astype(f32)).astype(bf16)
            b2_s[1] = (part[0, 2, RA + HB:S] + b1_r[2, HB:RB].astype(f32)).astype(bf16)
            b2 = [
                send(b2_s.at[0], b2_r.at[0], rs_send, rs_recv, 10, right),
                send(b2_s.at[1], b2_r.at[1], rs_send, rs_recv, 11, left),
            ]

    mass_twin.wait_recv()
    mass_s[1] = mass_s[0] + mass_r[0]
    mass_over = send(mass_s.at[1], mass_r.at[1], m_send, m_recv, 1, over)
    kc[3].wait_recv()
    kc.append(kkt_send(3, 1, half0, right, 7))
    kc[4].wait_recv()
    kc.append(kkt_send(1, 1, half1, left, 8))
    for copy in others:
        copy.wait()

    b1[1].wait_recv()
    b2[0].wait_recv()
    b3_s[0, 0:HB] = (
        part[0, 1, RA:RA + HB] + b1_r[1, 0:HB].astype(f32) + b2_r[0].astype(f32)
    ).astype(bf16)
    b3_s[0, HB:RB] = (part[0, 1, RA + HB:S] + b1_r[1, HB:RB].astype(f32)).astype(bf16)
    b3 = [send(b3_s.at[0], b3_r.at[0], rs_send, rs_recv, 12, right)]
    b1[3].wait_recv()
    b2[1].wait_recv()
    b3_s[1, 0:HB] = (part[0, 3, RA:RA + HB] + b1_r[3, 0:HB].astype(f32)).astype(bf16)
    b3_s[1, HB:RB] = (
        part[0, 3, RA + HB:S] + b1_r[3, HB:RB].astype(f32) + b2_r[1].astype(f32)
    ).astype(bf16)
    b3.append(send(b3_s.at[1], b3_r.at[1], rs_send, rs_recv, 13, left))

    a2[0, 1].wait_recv()
    a2[1, 1].wait_recv()
    a3_s[...] = (
        part[1, 0, 0:RA] + a2_r[0, 1].astype(f32) + a2_r[1, 1].astype(f32)
    ).astype(bf16)
    a3 = send(a3_s, a3_r, rs_send, rs_recv, 14, across)

    mass_over.wait_recv()
    mass_s[2] = mass_s[1] + mass_r[1]
    mass_z = [
        send(mass_s.at[2], mass_r.at[2], m_send, m_recv, 2, up),
        send(mass_s.at[2], mass_r.at[3], m_send, m_recv, 3, down),
    ]

    for k in range(5, 9):
        kc[k].wait_recv()

    @pl.loop(0, ROWS // CH)
    def _(j):
        rows = pl.ds(pl.multiple_of(j * CH, CH), CH)
        link[rows, piece] = nn(tech_v[rows, :], kkt_cols[...]).astype(bf16)

    def link_piece(oy, oz):
        return pl.ds(pl.multiple_of((peer_id(oy, oz) * 2 + core) * PIECE, PIECE), PIECE)

    def link_send(oy, oz, target, k):
        where = link.at[:, link_piece(oy, oz)]
        return send(where, where, l_send, l_recv, k, target)

    def twin_send(oy, oz, k):
        where = link.at[:, link_piece(oy, oz)]
        return send(where, where, t_send, t_recv, k, twin)

    mass_z[0].wait_recv()
    mass_z[1].wait_recv()
    mass_z.append(send(mass_s.at[2], mass_r.at[4], m_send, m_recv, 4, peer(0, 2)))
    lc = [
        link_send(0, 0, over, 0),
        link_send(0, 0, up, 1),
        link_send(0, 0, down, 2),
        link_send(0, 0, peer(0, 2), 3),
    ]
    tc = [twin_send(0, 0, 0)]

    demand_t = demand_v[...].T
    own = pl.ds(pl.multiple_of(d * B, B), B)
    b1[0].wait_recv()
    b3[0].wait_recv()
    b3[1].wait_recv()
    rhs[RA:S, own] = (
        demand_t[RA:S].astype(f32)
        - (
            part[0, 0, RA:S] + b1_r[0].astype(f32)
            + b3_r[0].astype(f32) + b3_r[1].astype(f32)
        )
    ).astype(bf16)

    low0, low1 = (0, HA), (HA, HA)
    low = (0, RA)
    high = (RA, RB)
    high0, high1 = (RA, HB), (RA + HB, HB)

    def gatherer(buf, ssem, rsem):
        def go(rows, dx, dy, target, k):
            cols = pl.ds(pl.multiple_of(dec_id(dx, dy) * B, B), B)
            where = buf.at[pl.ds(*rows), cols]
            return send(where, where, ssem, rsem, k, target)

        c = {}

        def start_high():
            c[0] = go(high, 0, 0, right, 0)
            c[1] = go(high, 0, 0, left, 1)
            c[2] = go(high, 0, 0, across, 2)

        def start_low():
            c[9] = go(low, 0, 0, across, 9)
            c[10] = go(low, 0, 0, right, 10)
            c[11] = go(low, 0, 0, left, 11)

        def first_turn():
            c[0].wait_recv()
            c[3] = go(high0, 3, 0, right, 3)
            c[5] = go(high, 3, 0, across, 5)
            c[1].wait_recv()
            c[4] = go(high1, 1, 0, left, 4)
            c[6] = go(high, 1, 0, across, 6)

        def rest():
            c[9].wait_recv()
            c[12] = go(low, 0, 1, right, 12)
            c[13] = go(low, 0, 1, left, 13)
            c[3].wait_recv()
            c[7] = go(high0, 2, 0, across, 7)
            c[4].wait_recv()
            c[8] = go(high1, 2, 0, across, 8)
            c[10].wait_recv()
            c[14] = go(low0, 3, 0, right, 14)
            c[11].wait_recv()
            c[15] = go(low1, 1, 0, left, 15)
            c[12].wait_recv()
            c[16] = go(low0, 3, 1, right, 16)
            c[13].wait_recv()
            c[17] = go(low1, 1, 1, left, 17)

        def end_high():
            for k in (2, 5, 6, 7, 8):
                c[k].wait_recv()

        def end_low():
            for k in (14, 15, 16, 17):
                c[k].wait_recv()

        return start_high, start_low, first_turn, rest, end_high, end_low

    high_1, low_1, turn_1, rest_1, end_high_1, end_low_1 = gatherer(rhs, ag1_send, ag1_recv)

    high_1()
    a2[0, 0].wait_recv()
    a2[1, 0].wait_recv()
    a3.wait_recv()
    rhs[0:RA, own] = (
        demand_t[0:RA].astype(f32)
        - (
            part[0, 0, 0:RA] + a2_r[0, 0].astype(f32)
            + a2_r[1, 0].astype(f32) + a3_r[...].astype(f32)
        )
    ).astype(bf16)
    low_1()
    lc[0].wait_recv()
    lc.append(link_send(1, 0, up, 4))
    lc.append(link_send(1, 0, down, 5))
    lc.append(link_send(1, 0, peer(0, 2), 6))
    tc.append(twin_send(1, 0, 1))
    turn_1()
    rest_1()
    for k, oz in ((1, 3), (2, 1), (3, 2)):
        lc[k].wait_recv()
        tc.append(twin_send(0, oz, 1 + k))
    end_high_1()
    end_low_1()
    for k, oz in ((4, 3), (5, 1), (6, 2)):
        lc[k].wait_recv()
        tc.append(twin_send(1, oz, 1 + k))
    for copy in tc:
        copy.wait_recv()

    def plan(rows):
        linked = nt(link[rows, :], rhs[...])
        gradient = cost_v[rows, :].astype(f32) + mult_v[rows, :] + linked
        planned = jnp.maximum(order_v[rows, :].astype(f32) - STEP * gradient, 0.0).astype(bf16)
        planned_v[rows, :] = planned
        return nt(planned, weight[...])

    def core_copy(j):
        return pltpu.make_async_remote_copy(
            src_ref=e1_s.at[j], dst_ref=e1_r.at[j],
            send_sem=e1_send.at[j], recv_sem=e1_recv.at[j],
            device_id=twin, device_id_type=MESH,
        )

    def slice_copy(oy, oz):
        k = oz * 2 + oy
        rows = pl.ds(pl.multiple_of(((yh + oy) % 2) * SLICE, SLICE), SLICE)
        return pltpu.make_async_remote_copy(
            src_ref=e2_s.at[oz, rows], dst_ref=e2_r.at[k],
            send_sem=e2_send.at[k], recv_sem=e2_recv.at[k],
            device_id=peer(oy, oz), device_id_type=MESH,
        )

    def core_rows(c):
        return pl.ds(pl.multiple_of(c * (CH // 2), CH // 2), CH // 2)

    def join(oz):
        core_copy(oz).wait_recv()
        total = tot[oz, core_rows(core), :] + e1_r[oz].astype(f32)
        tot[oz, core_rows(core), :] = total
        e2_s[oz] = total.astype(bf16)

    def compute(oz):
        tot[oz] = plan(pl.ds(pl.multiple_of(((z + oz) % 4) * CH, CH), CH))
        e1_s[oz] = tot[oz, core_rows(1 - core), :].astype(bf16)
        core_copy(oz).start()

    compute(3)

    @pl.loop(0, 3)
    def _(j):
        compute(2 - j)
        join(3 - j)
        slice_copy(0, 3 - j).start()
        slice_copy(1, 3 - j).start()

    join(0)
    slice_copy(1, 0).start()
    write_planned = pltpu.make_async_copy(planned_v, planned_out, out_sem.at[1])
    write_planned.start()
    rec_own[...] = nt(kkt_v[...], rhs[...]).astype(bf16)
    write_rec = pltpu.make_async_copy(rec_own, recourse_out, out_sem.at[0])
    write_rec.start()
    mass_z[2].wait_recv()
    mass = mass_s[2] + mass_r[2] + mass_r[3] + mass_r[4]
    total = tot[0, pl.ds(pl.multiple_of(core * (CH // 2) + yh * SLICE, SLICE), SLICE), :]
    for oy, oz in ((0, 3), (1, 3), (0, 2), (1, 2), (0, 1), (1, 1), (1, 0)):
        slice_copy(oy, oz).wait_recv()
        total = total + e2_r[oz * 2 + oy].astype(f32)

    def cons_at(oy, oz):
        first = ((z + oz) % 4) * CH + core * (CH // 2) + ((yh + oy) % 2) * SLICE
        return pl.ds(pl.multiple_of(first, SLICE), SLICE)

    mine = cons_at(0, 0)
    cons_b[mine, :] = (total / mass[0:1, :]).astype(bf16)
    f = [
        send(cons_b.at[mine], cons_b.at[mine], f_send, f_recv, k, peer(oy, oz))
        for k, (oy, oz) in enumerate(offsets)
    ]
    c = [send(cons_b.at[mine], cons_b.at[mine], c_send, c_recv, 7, twin)]
    for k, (oy, oz) in reversed(list(enumerate(offsets))):
        f[k].wait_recv()
        theirs = cons_at(oy, 4 - oz)
        c.append(send(cons_b.at[theirs], cons_b.at[theirs], c_send, c_recv, k, twin))
    for copy in c:
        copy.wait_recv()
    write_cons = pltpu.make_async_copy(cons_b, cons_out, out_sem.at[2])
    write_cons.start()

    for copy in started:
        copy.wait_send()
    for oz in range(4):
        core_copy(oz).wait_send()
        for oy in range(2):
            if oz or oy:
                slice_copy(oy, oz).wait_send()
    write_rec.wait()
    write_planned.wait()
    write_cons.wait()


def last_kernel(
    planned_hbm, recourse_hbm, cons_hbm, mult_hbm, node_ref,
    planned_out, recourse_out, cons_out, next_out,
    planned_v, recourse_v, cons_v, mult_v, cons_f, member, load, out_sem,
):
    pairs = ((planned_hbm, planned_v), (recourse_hbm, recourse_v), (cons_hbm, cons_v))
    loads = [pltpu.make_async_copy(a, b, load.at[k]) for k, (a, b) in enumerate(pairs)]
    loads.append(pltpu.make_async_copy(mult_hbm, mult_v, load.at[3]))
    for copy in loads:
        copy.start()
    node_ids = lax.broadcasted_iota(jnp.int32, (G, S), 0)
    member[...] = jnp.where(node_ids == node_ref[...], 1.0, 0.0).astype(bf16)
    loads[0].wait()
    writes = [pltpu.make_async_copy(planned_v, planned_out, out_sem.at[0])]
    writes[0].start()
    loads[1].wait()
    writes.append(pltpu.make_async_copy(recourse_v, recourse_out, out_sem.at[1]))
    writes[1].start()
    loads[2].wait()
    loads[3].wait()

    def put(j):
        rows = pl.ds(pl.multiple_of(j * CH, CH), CH)
        return (
            pltpu.make_async_copy(cons_f.at[rows], cons_out.at[rows], out_sem.at[2 + j]),
            pltpu.make_async_copy(mult_v.at[rows], next_out.at[rows], out_sem.at[6 + j]),
        )

    @pl.loop(0, ROWS // CH)
    def _(j):
        rows = pl.ds(pl.multiple_of(j * CH, CH), CH)
        spread = nn(cons_v[rows, :], member[...])
        cons_f[rows, :] = cons_v[rows, :].astype(f32)
        mult_v[rows, :] = mult_v[rows, :] + PENALTY * (planned_v[rows, :].astype(f32) - spread)
        for copy in put(j):
            copy.start()

    for copy in writes:
        copy.wait()
    for j in range(ROWS // CH):
        for copy in put(j):
            copy.wait()


def on_device(
    order_qty, multiplier, unit_cost, demand, technology, kkt_inverse, probability, scenario_node
):
    any_space = pl.BlockSpec(memory_space=pl.ANY)
    vmem = pl.BlockSpec(memory_space=pltpu.VMEM)
    hbm = pl.BlockSpec(memory_space=pltpu.HBM)
    V = pltpu.VMEM
    D = pltpu.SemaphoreType.DMA
    scratch = [
        V((ROWS, S), bf16), V((S, ROWS), bf16), V((ROWS, S), f32), V((ROWS, S), bf16),
        V((B, S), bf16), V((ROWS, M), bf16), V((B, M), bf16),
        V((2, 4, S, B), f32),
        V((2, 2, HA, B), bf16), V((2, 2, HA, B), bf16),
        V((2, 2, RA, B), bf16), V((2, 2, RA, B), bf16),
        V((RA, B), bf16), V((RA, B), bf16),
        V((4, RB, B), bf16), V((4, RB, B), bf16),
        V((2, HB, B), bf16), V((2, HB, B), bf16),
        V((2, RB, B), bf16), V((2, RB, B), bf16),
        V((S, M), bf16), V((ROWS, M), bf16), V((M, PIECE), bf16), V((B, S), bf16),
        V((G, S), bf16), V((3, 8, G), f32), V((5, 8, G), f32),
        V((ROWS, S), bf16), V((4, CH, G), f32),
        V((4, CH // 2, G), bf16), V((4, CH // 2, G), bf16),
        V((4, CH // 2, G), bf16), V((8, SLICE, G), bf16), V((ROWS, G), bf16),
        D((6,)), D((8,)), D((3,)),
        D((15,)), D((15,)), D((18,)), D((18,)), D((9,)), D((9,)), D((7,)), D((7,)), D((8,)), D((8,)),
        D((5,)), D((5,)), D((4,)), D((4,)), D((8,)), D((8,)), D((7,)), D((7,)), D((8,)), D((8,)),
    ]
    node_row = scenario_node.reshape(1, S)
    planned, recourse, consensus = pl.pallas_call(
        kernel,
        out_shape=(
            jax.ShapeDtypeStruct((ROWS, S), bf16),
            jax.ShapeDtypeStruct((B, S), bf16),
            jax.ShapeDtypeStruct((ROWS, G), bf16),
        ),
        in_specs=[any_space] * 6 + [vmem] * 2,
        out_specs=(any_space,) * 3,
        scratch_shapes=scratch,
        compiler_params=pltpu.CompilerParams(
            collective_id=0, has_side_effects=True, vmem_limit_bytes=56 * 2**20
        ),
    )(
        order_qty, multiplier, unit_cost, demand, technology, kkt_inverse,
        probability.reshape(1, S), node_row,
    )
    return tuple(
        pl.pallas_call(
            last_kernel,
            out_shape=(
                jax.ShapeDtypeStruct((ROWS, S), bf16),
                jax.ShapeDtypeStruct((B, S), bf16),
                jax.ShapeDtypeStruct((ROWS, G), f32),
                jax.ShapeDtypeStruct((ROWS, S), f32),
            ),
            in_specs=[hbm] * 4 + [vmem],
            out_specs=(any_space,) * 4,
            scratch_shapes=[
                V((ROWS, S), bf16), V((B, S), bf16), V((ROWS, G), bf16), V((ROWS, S), f32),
                V((ROWS, G), f32), V((G, S), bf16), D((4,)), D((10,)),
            ],
            compiler_params=pltpu.CompilerParams(vmem_limit_bytes=60 * 2**20),
        )(planned, recourse, consensus, multiplier, node_row)
    )


def solution(mesh):
    placed = (
        P("dec", "scen"),
        P("dec", "scen"),
        P("dec", "scen"),
        P("dec", "scen"),
        P("dec", None),
        P("dec", None),
        P("scen"),
        P("scen", None),
    )
    return jax.shard_map(
        on_device,
        mesh=mesh,
        in_specs=placed,
        out_specs=(P("dec", "scen"), P("dec", "scen"), P("dec", None), P("dec", "scen")),
        check_vma=False,
    )
```

```python
import jax
import jax.numpy as jnp
from jax import lax
from jax.experimental import pallas as pl
from jax.experimental.pallas import tpu as pltpu
from jax.sharding import PartitionSpec as P

G = 512
STEP = 0.5
PENALTY = 2.0

ROWS = 1024
S = 512
M = 2048
B = 256
SLICE = 64
CH = 256
PIECE = M // 16

RA = 288
HA = RA // 2
RB = S - RA
HB = RB // 2

bf16 = jnp.bfloat16
f32 = jnp.float32
MESH = pl.DeviceIdType.MESH


def nt(a, b):
    return lax.dot_general(a, b, (((1,), (1,)), ((), ())), preferred_element_type=f32)


def nn(a, b):
    return jnp.dot(a, b, preferred_element_type=f32)


def kernel(
    order_hbm, mult_hbm, cost_hbm, demand_hbm, tech_hbm, kkt_hbm, prob_ref, node_ref,
    planned_v, rec_own, cons_out,
    order_v, order_t, mult_v, cost_v, demand_v, tech_v, kkt_v,
    part,
    a1_s, a1_r, a2_s, a2_r, a3_s, a3_r,
    b1_s, b1_r, b2_s, b2_r, b3_s, b3_r,
    rhs, link, kkt_cols,
    weight, mass_s, mass_r,
    tot, e1_s, e1_r, e2_s, e2_r, cons_b,
    load, tload,
    rs_send, rs_recv, ag1_send, ag1_recv, k_send, k_recv, l_send, l_recv, t_send, t_recv,
    m_send, m_recv, e1_send, e1_recv, e2_send, e2_recv, f_send, f_recv, c_send, c_recv,
):
    s = lax.axis_index("scen")
    d = lax.axis_index("dec")
    x, y = d % 4, d // 4
    core, z, yh = s % 2, (s // 2) % 4, s // 8

    def dec_id(dx, dy):
        return ((y + dy) % 2) * 4 + (x + dx) % 4

    def peer_id(oy, oz):
        return ((yh + oy) % 2) * 4 + (z + oz) % 4

    right, left, across = (s, dec_id(1, 0)), (s, dec_id(3, 0)), (s, dec_id(0, 1))
    twin = (s - core + (1 - core), d)
    offsets = [(1, 2), (0, 2), (1, 1), (1, 3), (1, 0), (0, 1), (0, 3)]

    def peer(oy, oz):
        p = peer_id(oy, oz)
        return (p * 2 + core, d)

    up, down, over = peer(0, 1), peer(0, 3), peer(1, 0)

    barrier = pltpu.get_barrier_semaphore()
    beyond = (s, dec_id(2, 0))
    everyone = [right, left, across, twin, up, down, over, beyond]
    for other in everyone:
        pl.semaphore_signal(barrier, inc=1, device_id=other, device_id_type=MESH)

    started = []

    def send(src, dst, ssem, rsem, k, target):
        copy = pltpu.make_async_remote_copy(
            src_ref=src, dst_ref=dst, send_sem=ssem.at[k], recv_sem=rsem.at[k],
            device_id=target, device_id_type=MESH,
        )
        copy.start()
        started.append(copy)
        return copy

    piece = pl.ds(pl.multiple_of(s * PIECE, PIECE), PIECE)
    kkt_rows = pl.ds(pl.multiple_of(d * B, B), B)
    load_piece = pltpu.make_async_copy(
        kkt_hbm.at[:, piece], kkt_cols.at[kkt_rows, :], load.at[5]
    )
    load_piece.start()
    load_order = pltpu.make_async_copy(order_hbm, order_v, load.at[0])
    load_order.start()

    def tech_copy(r):
        dy, dx = tech_at(r)
        cols = pl.ds(pl.multiple_of(dec_id(dx, dy) * B, B), B)
        return pltpu.make_async_copy(tech_hbm.at[:, cols], tech_v.at[:, cols], tload.at[r])

    def tech_at(r):
        if r < 2:
            return 1 - r, 2
        return (1 if r < 5 else 0), (1 - (r - 2) % 3) % 4

    for r in range(8):
        tech_copy(r).start()
    others = [
        pltpu.make_async_copy(demand_hbm, demand_v, load.at[1]),
        pltpu.make_async_copy(kkt_hbm, kkt_v, load.at[2]),
        pltpu.make_async_copy(mult_hbm, mult_v, load.at[3]),
        pltpu.make_async_copy(cost_hbm, cost_v, load.at[4]),
    ]
    for copy in others:
        copy.start()

    node_ids = lax.broadcasted_iota(jnp.int32, (G, S), 0)
    weight[...] = jnp.where(node_ids == node_ref[...], prob_ref[...], 0.0).astype(bf16)
    mass_s[0] = nt(jnp.ones((16, S), bf16), weight[...])[0:8]
    load_order.wait()
    order_t[...] = order_v[...].T

    def first_product(dy, dx):
        cols = pl.ds(pl.multiple_of(dec_id(dx, dy) * B, B), B)
        part[dy, dx] = nn(order_t[...], tech_v[:, cols])

    tech_copy(0).wait()
    tech_copy(1).wait()

    @pl.loop(0, 2)
    def _(i):
        first_product(1 - i, 2)

    for dy in range(2):
        a1_s[0, dy] = part[dy, 2, 0:HA].astype(bf16)
        a1_s[1, dy] = part[dy, 2, HA:RA].astype(bf16)
    b1_s[2] = part[1, 2, RA:S].astype(bf16)

    pl.semaphore_wait(barrier, len(everyone))

    def kkt_send(dy, target, k):
        e = pl.ds(pl.multiple_of(dec_id(0, dy) * B, B), B)
        return send(kkt_cols.at[e, :], kkt_cols.at[e, :], k_send, k_recv, k, target)

    load_piece.wait()
    kc = [kkt_send(0, to, k) for k, to in enumerate((across, right, left, beyond))]
    a1 = [
        send(a1_s.at[0], a1_r.at[0], rs_send, rs_recv, 0, right),
        send(a1_s.at[1], a1_r.at[1], rs_send, rs_recv, 1, left),
    ]
    b1 = {2: send(b1_s.at[2], b1_r.at[2], rs_send, rs_recv, 2, across)}

    mass_twin = send(mass_s.at[0], mass_r.at[0], m_send, m_recv, 0, twin)
    for r in range(2, 5):
        tech_copy(r).wait()

    @pl.loop(0, 3)
    def _(i):
        first_product(1, (5 - i) % 4)

    for k, dx in enumerate((1, 3, 0)):
        b1_s[dx] = part[1, dx, RA:S].astype(bf16)
        b1[dx] = send(b1_s.at[dx], b1_r.at[dx], rs_send, rs_recv, 3 + k, across)

    for r in range(5, 8):
        tech_copy(r).wait()
    kc[0].wait_recv()
    for k, to in ((4, right), (5, left), (6, beyond)):
        kc.append(kkt_send(1, to, k))
    mass_twin.wait_recv()
    mass_s[1] = mass_s[0] + mass_r[0]
    mass_over = send(mass_s.at[1], mass_r.at[1], m_send, m_recv, 1, over)

    @pl.loop(0, 3)
    def _(i):
        first_product(0, (5 - i) % 4)

    a1[0].wait_recv()
    a1[1].wait_recv()
    a2 = {}
    for dy in (1, 0):
        a2_s[0, dy, 0:HA] = (part[dy, 1, 0:HA] + a1_r[0, dy].astype(f32)).astype(bf16)
        a2_s[0, dy, HA:RA] = part[dy, 1, HA:RA].astype(bf16)
        a2[0, dy] = send(a2_s.at[0, dy], a2_r.at[0, dy], rs_send, rs_recv, 6 + dy, right)
        a2_s[1, dy, 0:HA] = part[dy, 3, 0:HA].astype(bf16)
        a2_s[1, dy, HA:RA] = (part[dy, 3, HA:RA] + a1_r[1, dy].astype(f32)).astype(bf16)
        a2[1, dy] = send(a2_s.at[1, dy], a2_r.at[1, dy], rs_send, rs_recv, 8 + dy, left)
        if dy == 1:
            b1[2].wait_recv()
            b2_s[0] = (part[0, 2, RA:RA + HB] + b1_r[2, 0:HB].astype(f32)).astype(bf16)
            b2_s[1] = (part[0, 2, RA + HB:S] + b1_r[2, HB:RB].astype(f32)).astype(bf16)
            b2 = [
                send(b2_s.at[0], b2_r.at[0], rs_send, rs_recv, 10, right),
                send(b2_s.at[1], b2_r.at[1], rs_send, rs_recv, 11, left),
            ]

    for copy in others:
        copy.wait()

    mass_over.wait_recv()
    mass_s[2] = mass_s[1] + mass_r[1]
    mass_z = [
        send(mass_s.at[2], mass_r.at[2], m_send, m_recv, 2, up),
        send(mass_s.at[2], mass_r.at[3], m_send, m_recv, 3, down),
    ]
    demand_t = demand_v[...].T
    a2[0, 1].wait_recv()
    a2[1, 1].wait_recv()
    a3_s[...] = (
        part[1, 0, 0:RA] + a2_r[0, 1].astype(f32) + a2_r[1, 1].astype(f32)
    ).astype(bf16)
    a3 = send(a3_s, a3_r, rs_send, rs_recv, 14, across)

    b1[1].wait_recv()
    b2[0].wait_recv()
    b3_s[0, 0:HB] = (
        part[0, 1, RA:RA + HB] + b1_r[1, 0:HB].astype(f32) + b2_r[0].astype(f32)
    ).astype(bf16)
    b3_s[0, HB:RB] = (part[0, 1, RA + HB:S] + b1_r[1, HB:RB].astype(f32)).astype(bf16)
    b3 = [send(b3_s.at[0], b3_r.at[0], rs_send, rs_recv, 12, right)]
    b1[3].wait_recv()
    b2[1].wait_recv()
    b3_s[1, 0:HB] = (part[0, 3, RA:RA + HB] + b1_r[3, 0:HB].astype(f32)).astype(bf16)
    b3_s[1, HB:RB] = (
        part[0, 3, RA + HB:S] + b1_r[3, HB:RB].astype(f32) + b2_r[1].astype(f32)
    ).astype(bf16)
    b3.append(send(b3_s.at[1], b3_r.at[1], rs_send, rs_recv, 13, left))

    for k in range(1, 7):
        kc[k].wait_recv()

    @pl.loop(0, ROWS // CH)
    def _(j):
        rows = pl.ds(pl.multiple_of(j * CH, CH), CH)
        link[rows, piece] = nn(tech_v[rows, :], kkt_cols[...]).astype(bf16)

    def link_piece(oy, oz):
        return pl.ds(pl.multiple_of((peer_id(oy, oz) * 2 + core) * PIECE, PIECE), PIECE)

    def link_send(oy, oz, target, k):
        where = link.at[:, link_piece(oy, oz)]
        return send(where, where, l_send, l_recv, k, target)

    def twin_send(oy, oz, k):
        where = link.at[:, link_piece(oy, oz)]
        return send(where, where, t_send, t_recv, k, twin)

    mass_z[0].wait_recv()
    mass_z[1].wait_recv()
    mass_z.append(send(mass_s.at[2], mass_r.at[4], m_send, m_recv, 4, peer(0, 2)))
    lc = {k: link_send(0, 0, to, k) for k, to in ((1, up), (2, down), (3, peer(0, 2)))}
    tc = [twin_send(0, 0, 0)]
    lc[0] = link_send(0, 0, over, 0)

    own = pl.ds(pl.multiple_of(d * B, B), B)
    b1[0].wait_recv()
    b3[0].wait_recv()
    b3[1].wait_recv()
    rhs[RA:S, own] = (
        demand_t[RA:S].astype(f32)
        - (
            part[0, 0, RA:S] + b1_r[0].astype(f32)
            + b3_r[0].astype(f32) + b3_r[1].astype(f32)
        )
    ).astype(bf16)

    low0, low1 = (0, HA), (HA, HA)
    low = (0, RA)
    high = (RA, RB)
    high0, high1 = (RA, HB), (RA + HB, HB)

    def gatherer(buf, ssem, rsem):
        def go(rows, dx, dy, target, k):
            cols = pl.ds(pl.multiple_of(dec_id(dx, dy) * B, B), B)
            where = buf.at[pl.ds(*rows), cols]
            return send(where, where, ssem, rsem, k, target)

        c = {}

        def start_high():
            c[0] = go(high, 0, 0, right, 0)
            c[1] = go(high, 0, 0, left, 1)
            c[2] = go(high, 0, 0, across, 2)

        def start_low():
            c[9] = go(low, 0, 0, across, 9)
            c[10] = go(low, 0, 0, right, 10)
            c[11] = go(low, 0, 0, left, 11)

        def first_turn():
            c[0].wait_recv()
            c[3] = go(high0, 3, 0, right, 3)
            c[5] = go(high, 3, 0, across, 5)
            c[1].wait_recv()
            c[4] = go(high1, 1, 0, left, 4)
            c[6] = go(high, 1, 0, across, 6)

        def rest():
            c[9].wait_recv()
            c[12] = go(low, 0, 1, right, 12)
            c[13] = go(low, 0, 1, left, 13)
            c[3].wait_recv()
            c[7] = go(high0, 2, 0, across, 7)
            c[4].wait_recv()
            c[8] = go(high1, 2, 0, across, 8)
            c[10].wait_recv()
            c[14] = go(low0, 3, 0, right, 14)
            c[11].wait_recv()
            c[15] = go(low1, 1, 0, left, 15)
            c[12].wait_recv()
            c[16] = go(low0, 3, 1, right, 16)
            c[13].wait_recv()
            c[17] = go(low1, 1, 1, left, 17)

        def end_high():
            for k in (2, 5, 6, 7, 8):
                c[k].wait_recv()

        def end_low():
            for k in (14, 15, 16, 17):
                c[k].wait_recv()

        return start_high, start_low, first_turn, rest, end_high, end_low

    high_1, low_1, turn_1, rest_1, end_high_1, end_low_1 = gatherer(rhs, ag1_send, ag1_recv)

    high_1()
    a2[0, 0].wait_recv()
    a2[1, 0].wait_recv()
    a3.wait_recv()
    rhs[0:RA, own] = (
        demand_t[0:RA].astype(f32)
        - (
            part[0, 0, 0:RA] + a2_r[0, 0].astype(f32)
            + a2_r[1, 0].astype(f32) + a3_r[...].astype(f32)
        )
    ).astype(bf16)
    low_1()
    lc[0].wait_recv()
    lc[4] = link_send(1, 0, up, 4)
    lc[5] = link_send(1, 0, down, 5)
    lc[6] = link_send(1, 0, peer(0, 2), 6)
    tc.append(twin_send(1, 0, 1))
    turn_1()
    rest_1()
    for k, oz in ((1, 3), (2, 1), (3, 2)):
        lc[k].wait_recv()
        tc.append(twin_send(0, oz, 1 + k))
    end_high_1()
    end_low_1()
    for k, oz in ((4, 3), (5, 1), (6, 2)):
        lc[k].wait_recv()
        tc.append(twin_send(1, oz, 1 + k))
    for copy in tc:
        copy.wait_recv()

    def plan(rows):
        linked = nt(link[rows, :], rhs[...])
        gradient = cost_v[rows, :].astype(f32) + mult_v[rows, :] + linked
        planned = jnp.maximum(order_v[rows, :].astype(f32) - STEP * gradient, 0.0).astype(bf16)
        planned_v[rows, :] = planned
        return nt(planned, weight[...])

    def core_copy(j):
        return pltpu.make_async_remote_copy(
            src_ref=e1_s.at[j], dst_ref=e1_r.at[j],
            send_sem=e1_send.at[j], recv_sem=e1_recv.at[j],
            device_id=twin, device_id_type=MESH,
        )

    def slice_copy(oy, oz):
        k = oz * 2 + oy
        rows = pl.ds(pl.multiple_of(((yh + oy) % 2) * SLICE, SLICE), SLICE)
        return pltpu.make_async_remote_copy(
            src_ref=e2_s.at[oz, rows], dst_ref=e2_r.at[k],
            send_sem=e2_send.at[k], recv_sem=e2_recv.at[k],
            device_id=peer(oy, oz), device_id_type=MESH,
        )

    def core_rows(c):
        return pl.ds(pl.multiple_of(c * (CH // 2), CH // 2), CH // 2)

    def join(oz):
        core_copy(oz).wait_recv()
        total = tot[oz, core_rows(core), :] + e1_r[oz].astype(f32)
        tot[oz, core_rows(core), :] = total
        e2_s[oz] = total.astype(bf16)

    def compute(oz):
        tot[oz] = plan(pl.ds(pl.multiple_of(((z + oz) % 4) * CH, CH), CH))
        e1_s[oz] = tot[oz, core_rows(1 - core), :].astype(bf16)
        core_copy(oz).start()

    compute(3)

    @pl.loop(0, 3)
    def _(j):
        compute(2 - j)
        join(3 - j)
        slice_copy(0, 3 - j).start()
        slice_copy(1, 3 - j).start()

    join(0)
    slice_copy(1, 0).start()
    rec_own[...] = nt(kkt_v[...], rhs[...]).astype(bf16)
    mass_z[2].wait_recv()
    mass = mass_s[2] + mass_r[2] + mass_r[3] + mass_r[4]
    total = tot[0, pl.ds(pl.multiple_of(core * (CH // 2) + yh * SLICE, SLICE), SLICE), :]
    for oy, oz in ((0, 3), (1, 3), (0, 2), (1, 2), (0, 1), (1, 1), (1, 0)):
        slice_copy(oy, oz).wait_recv()
        total = total + e2_r[oz * 2 + oy].astype(f32)

    def cons_at(oy, oz):
        first = ((z + oz) % 4) * CH + core * (CH // 2) + ((yh + oy) % 2) * SLICE
        return pl.ds(pl.multiple_of(first, SLICE), SLICE)

    mine = cons_at(0, 0)
    cons_b[mine, :] = (total / mass[0:1, :]).astype(bf16)
    f = [
        send(cons_b.at[mine], cons_b.at[mine], f_send, f_recv, k, peer(oy, oz))
        for k, (oy, oz) in enumerate(offsets)
    ]
    c = [send(cons_b.at[mine], cons_b.at[mine], c_send, c_recv, 7, twin)]
    for k, (oy, oz) in reversed(list(enumerate(offsets))):
        f[k].wait_recv()
        theirs = cons_at(oy, 4 - oz)
        c.append(send(cons_b.at[theirs], cons_b.at[theirs], c_send, c_recv, k, twin))
    for copy in c:
        copy.wait_recv()
    cons_out[...] = cons_b[...]
    for copy in started:
        copy.wait_send()
    for oz in range(4):
        core_copy(oz).wait_send()
        for oy in range(2):
            if oz or oy:
                slice_copy(oy, oz).wait_send()


def last_kernel(
    planned_ref, recourse_ref, cons_ref, mult_ref, node_ref,
    planned_out, recourse_out, cons_out, next_out,
    cons_f, next_v, member, out_sem,
):
    writes = [
        pltpu.make_async_copy(planned_ref, planned_out, out_sem.at[0]),
        pltpu.make_async_copy(recourse_ref, recourse_out, out_sem.at[1]),
    ]
    for copy in writes:
        copy.start()
    node_ids = lax.broadcasted_iota(jnp.int32, (G, S), 0)
    member[...] = jnp.where(node_ids == node_ref[...], 1.0, 0.0).astype(bf16)

    def put(j):
        rows = pl.ds(pl.multiple_of(j * CH, CH), CH)
        return (
            pltpu.make_async_copy(cons_f.at[rows], cons_out.at[rows], out_sem.at[2 + j]),
            pltpu.make_async_copy(next_v.at[rows], next_out.at[rows], out_sem.at[6 + j]),
        )

    @pl.loop(0, ROWS // CH)
    def _(j):
        rows = pl.ds(pl.multiple_of(j * CH, CH), CH)
        spread = nn(cons_ref[rows, :], member[...])
        cons_f[rows, :] = cons_ref[rows, :].astype(f32)
        next_v[rows, :] = mult_ref[rows, :] + PENALTY * (
            planned_ref[rows, :].astype(f32) - spread
        )
        for copy in put(j):
            copy.start()

    for copy in writes:
        copy.wait()
    for j in range(ROWS // CH):
        for copy in put(j):
            copy.wait()


def on_device(
    order_qty, multiplier, unit_cost, demand, technology, kkt_inverse, probability, scenario_node
):
    any_space = pl.BlockSpec(memory_space=pl.ANY)
    vmem = pl.BlockSpec(memory_space=pltpu.VMEM)
    V = pltpu.VMEM
    D = pltpu.SemaphoreType.DMA
    scratch = [
        V((ROWS, S), bf16), V((S, ROWS), bf16), V((ROWS, S), f32), V((ROWS, S), bf16),
        V((B, S), bf16), V((ROWS, M), bf16), V((B, M), bf16),
        V((2, 4, S, B), f32),
        V((2, 2, HA, B), bf16), V((2, 2, HA, B), bf16),
        V((2, 2, RA, B), bf16), V((2, 2, RA, B), bf16),
        V((RA, B), bf16), V((RA, B), bf16),
        V((4, RB, B), bf16), V((4, RB, B), bf16),
        V((2, HB, B), bf16), V((2, HB, B), bf16),
        V((2, RB, B), bf16), V((2, RB, B), bf16),
        V((S, M), bf16), V((ROWS, M), bf16), V((M, PIECE), bf16),
        V((G, S), bf16), V((3, 8, G), f32), V((5, 8, G), f32),
        V((4, CH, G), f32),
        V((4, CH // 2, G), bf16), V((4, CH // 2, G), bf16),
        V((4, CH // 2, G), bf16), V((8, SLICE, G), bf16), V((ROWS, G), bf16),
        D((6,)), D((8,)),
        D((15,)), D((15,)), D((18,)), D((18,)), D((7,)), D((7,)), D((7,)), D((7,)), D((8,)), D((8,)),
        D((5,)), D((5,)), D((4,)), D((4,)), D((8,)), D((8,)), D((7,)), D((7,)), D((8,)), D((8,)),
    ]
    node_row = scenario_node.reshape(1, S)
    planned, recourse, consensus = pl.pallas_call(
        kernel,
        out_shape=(V((ROWS, S), bf16), V((B, S), bf16), V((ROWS, G), bf16)),
        in_specs=[any_space] * 6 + [vmem] * 2,
        out_specs=(vmem,) * 3,
        scratch_shapes=scratch,
        compiler_params=pltpu.CompilerParams(
            collective_id=0, has_side_effects=True, vmem_limit_bytes=57 * 2**20
        ),
    )(
        order_qty, multiplier, unit_cost, demand, technology, kkt_inverse,
        probability.reshape(1, S), node_row,
    )
    return tuple(
        pl.pallas_call(
            last_kernel,
            out_shape=(
                jax.ShapeDtypeStruct((ROWS, S), bf16),
                jax.ShapeDtypeStruct((B, S), bf16),
                jax.ShapeDtypeStruct((ROWS, G), f32),
                jax.ShapeDtypeStruct((ROWS, S), f32),
            ),
            in_specs=[vmem] * 5,
            out_specs=(any_space,) * 4,
            scratch_shapes=[
                V((ROWS, G), f32), V((ROWS, S), f32), V((G, S), bf16), D((10,)),
            ],
            compiler_params=pltpu.CompilerParams(vmem_limit_bytes=24 * 2**20),
        )(planned, recourse, consensus, multiplier, node_row)
    )


def solution(mesh):
    placed = (
        P("dec", "scen"),
        P("dec", "scen"),
        P("dec", "scen"),
        P("dec", "scen"),
        P("dec", None),
        P("dec", None),
        P("scen"),
        P("scen", None),
    )
    return jax.shard_map(
        on_device,
        mesh=mesh,
        in_specs=placed,
        out_specs=(P("dec", "scen"), P("dec", "scen"), P("dec", None), P("dec", "scen")),
        check_vma=False,
    )
```

```python
import jax
import jax.numpy as jnp
from jax import lax
from jax.experimental import pallas as pl
from jax.experimental.pallas import tpu as pltpu
from jax.sharding import PartitionSpec as P

G = 512
STEP = 0.5
PENALTY = 2.0

ROWS = 1024
S = 512
M = 2048
B = 256
SLICE = 64
CH = 256
PIECE = M // 16

RA = 256
HA = RA // 2
RB = S - RA
HB = RB // 2

bf16 = jnp.bfloat16
f32 = jnp.float32
MESH = pl.DeviceIdType.MESH


def nt(a, b):
    return lax.dot_general(a, b, (((1,), (1,)), ((), ())), preferred_element_type=f32)


def nn(a, b):
    return jnp.dot(a, b, preferred_element_type=f32)


def kernel(
    order_hbm, mult_hbm, cost_hbm, demand_hbm, tech_hbm, kkt_hbm, prob_ref, node_ref,
    planned_v, rec_own, cons_out,
    order_v, order_t, mult_v, cost_v, demand_v, tech_v, kkt_v,
    part,
    a1_s, a1_r, a2_s, a2_r, a3_s, a3_r,
    b1_s, b1_r, b2_s, b2_r, b3_s, b3_r,
    rhs, link, kkt_cols, known,
    weight, mass_s, mass_r,
    tot, e1_s, e1_r, e2_s, e2_r, cons_b,
    load, tload,
    rs_send, rs_recv, ag1_send, ag1_recv, k_send, k_recv, l_send, l_recv, t_send, t_recv,
    m_send, m_recv, e1_send, e1_recv, e2_send, e2_recv, f_send, f_recv, c_send, c_recv,
):
    s = lax.axis_index("scen")
    d = lax.axis_index("dec")
    x, y = d % 4, d // 4
    core, z, yh = s % 2, (s // 2) % 4, s // 8

    def dec_id(dx, dy):
        return ((y + dy) % 2) * 4 + (x + dx) % 4

    def peer_id(oy, oz):
        return ((yh + oy) % 2) * 4 + (z + oz) % 4

    right, left, across = (s, dec_id(1, 0)), (s, dec_id(3, 0)), (s, dec_id(0, 1))
    twin = (s - core + (1 - core), d)
    offsets = [(1, 2), (0, 2), (1, 1), (1, 3), (1, 0), (0, 1), (0, 3)]

    def peer(oy, oz):
        p = peer_id(oy, oz)
        return (p * 2 + core, d)

    up, down, over = peer(0, 1), peer(0, 3), peer(1, 0)

    barrier = pltpu.get_barrier_semaphore()
    beyond = (s, dec_id(2, 0))
    everyone = [right, left, across, twin, up, down, over, beyond]
    for other in everyone:
        pl.semaphore_signal(barrier, inc=1, device_id=other, device_id_type=MESH)

    started = []

    def send(src, dst, ssem, rsem, k, target):
        copy = pltpu.make_async_remote_copy(
            src_ref=src, dst_ref=dst, send_sem=ssem.at[k], recv_sem=rsem.at[k],
            device_id=target, device_id_type=MESH,
        )
        copy.start()
        started.append(copy)
        return copy

    piece = pl.ds(pl.multiple_of(s * PIECE, PIECE), PIECE)
    kkt_rows = pl.ds(pl.multiple_of(d * B, B), B)
    load_piece = pltpu.make_async_copy(
        kkt_hbm.at[:, piece], kkt_cols.at[kkt_rows, :], load.at[5]
    )
    load_piece.start()
    load_order = pltpu.make_async_copy(order_hbm, order_v, load.at[0])
    load_order.start()

    def tech_copy(r):
        dy, dx = tech_at(r)
        cols = pl.ds(pl.multiple_of(dec_id(dx, dy) * B, B), B)
        return pltpu.make_async_copy(tech_hbm.at[:, cols], tech_v.at[:, cols], tload.at[r])

    def tech_at(r):
        if r < 2:
            return 1 - r, 2
        return (1 if r < 5 else 0), (1 - (r - 2) % 3) % 4

    for r in range(8):
        tech_copy(r).start()
    others = [
        pltpu.make_async_copy(demand_hbm, demand_v, load.at[1]),
        pltpu.make_async_copy(kkt_hbm, kkt_v, load.at[2]),
        pltpu.make_async_copy(mult_hbm, mult_v, load.at[3]),
        pltpu.make_async_copy(cost_hbm, cost_v, load.at[4]),
    ]
    for copy in others:
        copy.start()

    node_ids = lax.broadcasted_iota(jnp.int32, (G, S), 0)
    weight[...] = jnp.where(node_ids == node_ref[...], prob_ref[...], 0.0).astype(bf16)
    mass_s[0] = nt(jnp.ones((16, S), bf16), weight[...])[0:8]
    load_order.wait()
    order_t[...] = order_v[...].T

    def first_product(dy, dx):
        cols = pl.ds(pl.multiple_of(dec_id(dx, dy) * B, B), B)
        part[dy, dx] = nn(order_t[...], tech_v[:, cols])

    tech_copy(0).wait()
    tech_copy(1).wait()

    @pl.loop(0, 2)
    def _(i):
        first_product(1 - i, 2)

    for dy in range(2):
        a1_s[0, dy] = part[dy, 2, 0:HA].astype(bf16)
        a1_s[1, dy] = part[dy, 2, HA:RA].astype(bf16)
    b1_s[2] = part[1, 2, RA:S].astype(bf16)

    pl.semaphore_wait(barrier, len(everyone))

    def kkt_send(dy, target, k):
        e = pl.ds(pl.multiple_of(dec_id(0, dy) * B, B), B)
        return send(kkt_cols.at[e, :], kkt_cols.at[e, :], k_send, k_recv, k, target)

    load_piece.wait()
    kc = [kkt_send(0, to, k) for k, to in enumerate((across, right, left, beyond))]
    a1 = [
        send(a1_s.at[0], a1_r.at[0], rs_send, rs_recv, 0, right),
        send(a1_s.at[1], a1_r.at[1], rs_send, rs_recv, 1, left),
    ]
    b1 = {2: send(b1_s.at[2], b1_r.at[2], rs_send, rs_recv, 2, across)}

    mass_twin = send(mass_s.at[0], mass_r.at[0], m_send, m_recv, 0, twin)
    for r in range(2, 5):
        tech_copy(r).wait()

    @pl.loop(0, 3)
    def _(i):
        first_product(1, (5 - i) % 4)

    for k, dx in enumerate((1, 3, 0)):
        b1_s[dx] = part[1, dx, RA:S].astype(bf16)
        b1[dx] = send(b1_s.at[dx], b1_r.at[dx], rs_send, rs_recv, 3 + k, across)

    for r in range(5, 8):
        tech_copy(r).wait()
    kc[0].wait_recv()
    for k, to in ((4, right), (5, left), (6, beyond)):
        kc.append(kkt_send(1, to, k))
    mass_twin.wait_recv()
    mass_s[1] = mass_s[0] + mass_r[0]
    mass_over = send(mass_s.at[1], mass_r.at[1], m_send, m_recv, 1, over)

    @pl.loop(0, 3)
    def _(i):
        first_product(0, (5 - i) % 4)

    a1[0].wait_recv()
    a1[1].wait_recv()
    a2 = {}
    for dy in (1, 0):
        a2_s[0, dy, 0:HA] = (part[dy, 1, 0:HA] + a1_r[0, dy].astype(f32)).astype(bf16)
        a2_s[0, dy, HA:RA] = part[dy, 1, HA:RA].astype(bf16)
        a2[0, dy] = send(a2_s.at[0, dy], a2_r.at[0, dy], rs_send, rs_recv, 6 + dy, right)
        a2_s[1, dy, 0:HA] = part[dy, 3, 0:HA].astype(bf16)
        a2_s[1, dy, HA:RA] = (part[dy, 3, HA:RA] + a1_r[1, dy].astype(f32)).astype(bf16)
        a2[1, dy] = send(a2_s.at[1, dy], a2_r.at[1, dy], rs_send, rs_recv, 8 + dy, left)
        if dy == 1:
            b1[2].wait_recv()
            b2_s[0] = (part[0, 2, RA:RA + HB] + b1_r[2, 0:HB].astype(f32)).astype(bf16)
            b2_s[1] = (part[0, 2, RA + HB:S] + b1_r[2, HB:RB].astype(f32)).astype(bf16)
            b2 = [
                send(b2_s.at[0], b2_r.at[0], rs_send, rs_recv, 10, right),
                send(b2_s.at[1], b2_r.at[1], rs_send, rs_recv, 11, left),
            ]

    for copy in others:
        copy.wait()

    mass_over.wait_recv()
    mass_s[2] = mass_s[1] + mass_r[1]
    mass_z = [
        send(mass_s.at[2], mass_r.at[2], m_send, m_recv, 2, up),
        send(mass_s.at[2], mass_r.at[3], m_send, m_recv, 3, down),
    ]
    demand_t = demand_v[...].T
    a2[0, 1].wait_recv()
    a2[1, 1].wait_recv()
    a3_s[...] = (
        part[1, 0, 0:RA] + a2_r[0, 1].astype(f32) + a2_r[1, 1].astype(f32)
    ).astype(bf16)
    a3 = send(a3_s, a3_r, rs_send, rs_recv, 14, across)

    b1[1].wait_recv()
    b2[0].wait_recv()
    b3_s[0, 0:HB] = (
        part[0, 1, RA:RA + HB] + b1_r[1, 0:HB].astype(f32) + b2_r[0].astype(f32)
    ).astype(bf16)
    b3_s[0, HB:RB] = (part[0, 1, RA + HB:S] + b1_r[1, HB:RB].astype(f32)).astype(bf16)
    b3 = [send(b3_s.at[0], b3_r.at[0], rs_send, rs_recv, 12, right)]
    b1[3].wait_recv()
    b2[1].wait_recv()
    b3_s[1, 0:HB] = (part[0, 3, RA:RA + HB] + b1_r[3, 0:HB].astype(f32)).astype(bf16)
    b3_s[1, HB:RB] = (
        part[0, 3, RA + HB:S] + b1_r[3, HB:RB].astype(f32) + b2_r[1].astype(f32)
    ).astype(bf16)
    b3.append(send(b3_s.at[1], b3_r.at[1], rs_send, rs_recv, 13, left))

    for k in range(1, 7):
        kc[k].wait_recv()

    @pl.loop(0, ROWS // CH)
    def _(j):
        rows = pl.ds(pl.multiple_of(j * CH, CH), CH)
        link[rows, piece] = nn(tech_v[rows, :], kkt_cols[...]).astype(bf16)

    def link_piece(oy, oz):
        return pl.ds(pl.multiple_of((peer_id(oy, oz) * 2 + core) * PIECE, PIECE), PIECE)

    def link_send(oy, oz, target, k):
        where = link.at[:, link_piece(oy, oz)]
        return send(where, where, l_send, l_recv, k, target)

    def twin_send(oy, oz, k):
        where = link.at[:, link_piece(oy, oz)]
        return send(where, where, t_send, t_recv, k, twin)

    mass_z[0].wait_recv()
    mass_z[1].wait_recv()
    mass_z.append(send(mass_s.at[2], mass_r.at[4], m_send, m_recv, 4, peer(0, 2)))
    lc = {k: link_send(0, 0, to, k) for k, to in ((1, up), (2, down), (3, peer(0, 2)))}
    tc = [twin_send(0, 0, 0)]
    lc[0] = link_send(0, 0, over, 0)

    own = pl.ds(pl.multiple_of(d * B, B), B)
    b1[0].wait_recv()
    b3[0].wait_recv()
    b3[1].wait_recv()
    rhs[RA:S, own] = (
        demand_t[RA:S].astype(f32)
        - (
            part[0, 0, RA:S] + b1_r[0].astype(f32)
            + b3_r[0].astype(f32) + b3_r[1].astype(f32)
        )
    ).astype(bf16)

    low0, low1 = (0, HA), (HA, HA)
    low = (0, RA)
    high = (RA, RB)
    high0, high1 = (RA, HB), (RA + HB, HB)

    def gatherer(buf, ssem, rsem):
        def go(rows, dx, dy, target, k):
            cols = pl.ds(pl.multiple_of(dec_id(dx, dy) * B, B), B)
            where = buf.at[pl.ds(*rows), cols]
            return send(where, where, ssem, rsem, k, target)

        c = {}

        def start_high():
            c[0] = go(high, 0, 0, right, 0)
            c[1] = go(high, 0, 0, left, 1)
            c[2] = go(high, 0, 0, across, 2)

        def start_low():
            c[9] = go(low, 0, 0, across, 9)
            c[10] = go(low, 0, 0, right, 10)
            c[11] = go(low, 0, 0, left, 11)

        def first_turn():
            c[0].wait_recv()
            c[3] = go(high0, 3, 0, right, 3)
            c[5] = go(high, 3, 0, across, 5)
            c[1].wait_recv()
            c[4] = go(high1, 1, 0, left, 4)
            c[6] = go(high, 1, 0, across, 6)

        def rest():
            c[9].wait_recv()
            c[12] = go(low, 0, 1, right, 12)
            c[13] = go(low, 0, 1, left, 13)
            c[3].wait_recv()
            c[7] = go(high0, 2, 0, across, 7)
            c[4].wait_recv()
            c[8] = go(high1, 2, 0, across, 8)
            c[10].wait_recv()
            c[14] = go(low0, 3, 0, right, 14)
            c[11].wait_recv()
            c[15] = go(low1, 1, 0, left, 15)
            c[12].wait_recv()
            c[16] = go(low0, 3, 1, right, 16)
            c[13].wait_recv()
            c[17] = go(low1, 1, 1, left, 17)

        def end_high():
            for k in (2, 5, 6, 7, 8):
                c[k].wait_recv()

        def end_low():
            for k in (14, 15, 16, 17):
                c[k].wait_recv()

        return start_high, start_low, first_turn, rest, end_high, end_low

    high_1, low_1, turn_1, rest_1, end_high_1, end_low_1 = gatherer(rhs, ag1_send, ag1_recv)

    high_1()
    a2[0, 0].wait_recv()
    a2[1, 0].wait_recv()
    a3.wait_recv()
    rhs[0:RA, own] = (
        demand_t[0:RA].astype(f32)
        - (
            part[0, 0, 0:RA] + a2_r[0, 0].astype(f32)
            + a2_r[1, 0].astype(f32) + a3_r[...].astype(f32)
        )
    ).astype(bf16)
    low_1()

    @pl.loop(0, ROWS // CH)
    def _(j):
        rows = pl.ds(pl.multiple_of(j * CH, CH), CH)
        known[rows, :] = order_v[rows, :].astype(f32) - STEP * (
            cost_v[rows, :].astype(f32) + mult_v[rows, :]
        )

    lc[0].wait_recv()
    lc[4] = link_send(1, 0, up, 4)
    lc[5] = link_send(1, 0, down, 5)
    lc[6] = link_send(1, 0, peer(0, 2), 6)
    tc.append(twin_send(1, 0, 1))
    turn_1()
    rest_1()
    for k, oz in ((1, 3), (2, 1), (3, 2)):
        lc[k].wait_recv()
        tc.append(twin_send(0, oz, 1 + k))
    end_high_1()
    end_low_1()
    for k, oz in ((4, 3), (5, 1), (6, 2)):
        lc[k].wait_recv()
        tc.append(twin_send(1, oz, 1 + k))
    for copy in tc:
        copy.wait_recv()

    def plan(rows):
        linked = nt(link[rows, :], rhs[...])
        planned = jnp.maximum(known[rows, :] - STEP * linked, 0.0).astype(bf16)
        planned_v[rows, :] = planned
        return nt(planned, weight[...])

    def core_copy(j):
        return pltpu.make_async_remote_copy(
            src_ref=e1_s.at[j], dst_ref=e1_r.at[j],
            send_sem=e1_send.at[j], recv_sem=e1_recv.at[j],
            device_id=twin, device_id_type=MESH,
        )

    def slice_copy(oy, oz):
        k = oz * 2 + oy
        rows = pl.ds(pl.multiple_of(((yh + oy) % 2) * SLICE, SLICE), SLICE)
        return pltpu.make_async_remote_copy(
            src_ref=e2_s.at[oz, rows], dst_ref=e2_r.at[k],
            send_sem=e2_send.at[k], recv_sem=e2_recv.at[k],
            device_id=peer(oy, oz), device_id_type=MESH,
        )

    def core_rows(c):
        return pl.ds(pl.multiple_of(c * (CH // 2), CH // 2), CH // 2)

    def join(oz):
        core_copy(oz).wait_recv()
        total = tot[oz, core_rows(core), :] + e1_r[oz].astype(f32)
        tot[oz, core_rows(core), :] = total
        e2_s[oz] = total.astype(bf16)

    def compute(oz):
        tot[oz] = plan(pl.ds(pl.multiple_of(((z + oz) % 4) * CH, CH), CH))
        e1_s[oz] = tot[oz, core_rows(1 - core), :].astype(bf16)
        core_copy(oz).start()

    compute(3)

    @pl.loop(0, 3)
    def _(j):
        compute(2 - j)
        join(3 - j)
        slice_copy(0, 3 - j).start()
        slice_copy(1, 3 - j).start()

    join(0)
    slice_copy(1, 0).start()
    rec_own[...] = nt(kkt_v[...], rhs[...]).astype(bf16)
    mass_z[2].wait_recv()
    mass = mass_s[2] + mass_r[2] + mass_r[3] + mass_r[4]
    total = tot[0, pl.ds(pl.multiple_of(core * (CH // 2) + yh * SLICE, SLICE), SLICE), :]
    for oy, oz in ((0, 3), (1, 3), (0, 2), (1, 2), (0, 1), (1, 1), (1, 0)):
        slice_copy(oy, oz).wait_recv()
        total = total + e2_r[oz * 2 + oy].astype(f32)

    def cons_at(oy, oz):
        first = ((z + oz) % 4) * CH + core * (CH // 2) + ((yh + oy) % 2) * SLICE
        return pl.ds(pl.multiple_of(first, SLICE), SLICE)

    mine = cons_at(0, 0)
    cons_b[mine, :] = (total / mass[0:1, :]).astype(bf16)
    f = [
        send(cons_b.at[mine], cons_b.at[mine], f_send, f_recv, k, peer(oy, oz))
        for k, (oy, oz) in enumerate(offsets)
    ]
    c = [send(cons_b.at[mine], cons_b.at[mine], c_send, c_recv, 7, twin)]
    for k, (oy, oz) in reversed(list(enumerate(offsets))):
        f[k].wait_recv()
        theirs = cons_at(oy, 4 - oz)
        c.append(send(cons_b.at[theirs], cons_b.at[theirs], c_send, c_recv, k, twin))
    for copy in c:
        copy.wait_recv()
    cons_out[...] = cons_b[...]
    for copy in started:
        copy.wait_send()
    for oz in range(4):
        core_copy(oz).wait_send()
        for oy in range(2):
            if oz or oy:
                slice_copy(oy, oz).wait_send()


def last_kernel(
    planned_ref, recourse_ref, cons_ref, mult_ref, node_ref,
    planned_out, recourse_out, cons_out, next_out,
    cons_f, next_v, member, out_sem,
):
    writes = [
        pltpu.make_async_copy(planned_ref, planned_out, out_sem.at[0]),
        pltpu.make_async_copy(recourse_ref, recourse_out, out_sem.at[1]),
    ]
    for copy in writes:
        copy.start()
    node_ids = lax.broadcasted_iota(jnp.int32, (G, S), 0)
    member[...] = jnp.where(node_ids == node_ref[...], 1.0, 0.0).astype(bf16)

    def put(j):
        rows = pl.ds(pl.multiple_of(j * CH, CH), CH)
        return (
            pltpu.make_async_copy(cons_f.at[rows], cons_out.at[rows], out_sem.at[2 + j]),
            pltpu.make_async_copy(next_v.at[rows], next_out.at[rows], out_sem.at[6 + j]),
        )

    @pl.loop(0, ROWS // CH)
    def _(j):
        rows = pl.ds(pl.multiple_of(j * CH, CH), CH)
        spread = nn(cons_ref[rows, :], member[...])
        cons_f[rows, :] = cons_ref[rows, :].astype(f32)
        next_v[rows, :] = mult_ref[rows, :] + PENALTY * (
            planned_ref[rows, :].astype(f32) - spread
        )
        for copy in put(j):
            copy.start()

    for copy in writes:
        copy.wait()
    for j in range(ROWS // CH):
        for copy in put(j):
            copy.wait()


def on_device(
    order_qty, multiplier, unit_cost, demand, technology, kkt_inverse, probability, scenario_node
):
    any_space = pl.BlockSpec(memory_space=pl.ANY)
    vmem = pl.BlockSpec(memory_space=pltpu.VMEM)
    V = pltpu.VMEM
    D = pltpu.SemaphoreType.DMA
    scratch = [
        V((ROWS, S), bf16), V((S, ROWS), bf16), V((ROWS, S), f32), V((ROWS, S), bf16),
        V((B, S), bf16), V((ROWS, M), bf16), V((B, M), bf16),
        V((2, 4, S, B), f32),
        V((2, 2, HA, B), bf16), V((2, 2, HA, B), bf16),
        V((2, 2, RA, B), bf16), V((2, 2, RA, B), bf16),
        V((RA, B), bf16), V((RA, B), bf16),
        V((4, RB, B), bf16), V((4, RB, B), bf16),
        V((2, HB, B), bf16), V((2, HB, B), bf16),
        V((2, RB, B), bf16), V((2, RB, B), bf16),
        V((S, M), bf16), V((ROWS, M), bf16), V((M, PIECE), bf16), V((ROWS, S), f32),
        V((G, S), bf16), V((3, 8, G), f32), V((5, 8, G), f32),
        V((4, CH, G), f32),
        V((4, CH // 2, G), bf16), V((4, CH // 2, G), bf16),
        V((4, CH // 2, G), bf16), V((8, SLICE, G), bf16), V((ROWS, G), bf16),
        D((6,)), D((8,)),
        D((15,)), D((15,)), D((18,)), D((18,)), D((7,)), D((7,)), D((7,)), D((7,)), D((8,)), D((8,)),
        D((5,)), D((5,)), D((4,)), D((4,)), D((8,)), D((8,)), D((7,)), D((7,)), D((8,)), D((8,)),
    ]
    node_row = scenario_node.reshape(1, S)
    planned, recourse, consensus = pl.pallas_call(
        kernel,
        out_shape=(V((ROWS, S), bf16), V((B, S), bf16), V((ROWS, G), bf16)),
        in_specs=[any_space] * 6 + [vmem] * 2,
        out_specs=(vmem,) * 3,
        scratch_shapes=scratch,
        compiler_params=pltpu.CompilerParams(
            collective_id=0, has_side_effects=True, vmem_limit_bytes=57 * 2**20
        ),
    )(
        order_qty, multiplier, unit_cost, demand, technology, kkt_inverse,
        probability.reshape(1, S), node_row,
    )
    return tuple(
        pl.pallas_call(
            last_kernel,
            out_shape=(
                jax.ShapeDtypeStruct((ROWS, S), bf16),
                jax.ShapeDtypeStruct((B, S), bf16),
                jax.ShapeDtypeStruct((ROWS, G), f32),
                jax.ShapeDtypeStruct((ROWS, S), f32),
            ),
            in_specs=[vmem] * 5,
            out_specs=(any_space,) * 4,
            scratch_shapes=[
                V((ROWS, G), f32), V((ROWS, S), f32), V((G, S), bf16), D((10,)),
            ],
            compiler_params=pltpu.CompilerParams(vmem_limit_bytes=24 * 2**20),
        )(planned, recourse, consensus, multiplier, node_row)
    )


def solution(mesh):
    placed = (
        P("dec", "scen"),
        P("dec", "scen"),
        P("dec", "scen"),
        P("dec", "scen"),
        P("dec", None),
        P("dec", None),
        P("scen"),
        P("scen", None),
    )
    return jax.shard_map(
        on_device,
        mesh=mesh,
        in_specs=placed,
        out_specs=(P("dec", "scen"), P("dec", "scen"), P("dec", None), P("dec", "scen")),
        check_vma=False,
    )
```
